128 devices in a mesh: dp: 8 (over y, core), fsdp: 16 (over z, x).
Axes of the slice: x: 4, y: 4, z: 4, core: 2. Of those that a mesh axis runs over, the one named last changes fastest.
Arguments:
- attn_out: bfloat16 [32768, 3072], P(('dp', 'fsdp')), may hold values from -0.078125 to 0.078125
- out_grad: bfloat16 [32768, 3072], P(('dp', 'fsdp')), may hold values from -24 to 24
- weight: bfloat16 [3072, 3072], P('fsdp'), may hold values from -0.109375 to 0.109375
- sign_vector: int32 [3072], replicated, may hold values from -1 to 1, as said below
Outputs:
- input_grad: bfloat16 [32768, 3072], P(('dp', 'fsdp'))
- weight_grad: float32 [3072, 3072], P('fsdp', 'dp')
The draws below stay inside these ranges and needn't reach their ends.
Inputs may be any that keep to these rules, and one draw needn't show every extreme that they name: `sign_vector`: each entry is -1 or +1.
All inputs are finite; a program needn't handle non-finite values.
Results may differ from the reference program's by a relative error of at most 0.004.
Values may be sent and summed in bfloat16 or wider, within the bound.
A program may use at most 128 MiB of HBM per device.

```python
import math
import jax
import jax.numpy as jnp
from jax import lax

HD = 3072
DW = 3072
BLOCK = 128
ALLTOK = 32768
N_DP = 8


def draw_sign_vector(key, part):
    key = jax.random.fold_in(key, 3)
    return 2 * jax.random.randint(key, (DW,), 0, 2, dtype=jnp.int32) - 1


def raised(array, own_key, source, target, shards_of, factor):
    owner, partner = [(jnp.arange(array.shape[dim]) // (array.shape[dim] // shards_of)).reshape([-1 if axis == dim else 1 for axis in range(array.ndim)]) for dim in (source, target)]
    chosen = jax.random.permutation(own_key, shards_of)[partner]
    strong = (owner == chosen) | (owner == (partner + shards_of // 2) % shards_of)
    return jnp.where(strong, factor * array, array)


def shard_levels(key, shape, cuts, low, top_value):
    loudness, own = 1.0, jax.random.fold_in(key, 6)
    for dim, blocks in cuts:
        steps = jnp.exp(jax.random.uniform(jax.random.fold_in(own, dim), (blocks,), jnp.float32, low / len(cuts), top_value / len(cuts)))
        loudness = loudness * jnp.repeat(steps, shape[dim] // blocks).reshape([-1 if axis == dim else 1 for axis in range(len(shape))])
    return loudness


def normal_values(key, dims, deviation, reach, shards=(), kind=jnp.bfloat16):
    drawn = deviation * jax.random.normal(key, dims, jnp.float32)
    if shards:
        drawn = drawn * shard_levels(key, dims, shards, -0.22, 0.18)
    return jnp.clip(drawn, -reach, reach).astype(kind)


def noise_with(key, dims, width, reach, cuts, heavy, kind=jnp.bfloat16):
    drawn = width * jax.random.normal(key, dims, jnp.float32)
    if cuts:
        drawn = drawn * shard_levels(key, dims, cuts, -0.22, 0.18)
    return jnp.clip(raised(drawn, jax.random.fold_in(key, 3), *heavy), -reach, reach).astype(kind)


def setup_inputs(seed: int = 0) -> dict:
    key_list = jax.random.split(jax.random.key(seed), 5)
    return {
        "attn_out": normal_values(key_list[0], (ALLTOK, HD), (ALLTOK ** -0.5), 0.078125, ((0, 128),)),
        "out_grad": noise_with(key_list[1], (ALLTOK, DW), 1.0, 24.0, ((0, 128),), (0, 1, 128, 5.5)),
        "weight": normal_values(key_list[2], (HD, DW), DW ** -0.5, 0.109375, ((0, 16),)),
        "sign_vector": draw_sign_vector(jax.random.fold_in(key_list[4], 71), 0),
    }


EPSILON = 1e-06

def hadamard():
    position = jnp.arange(BLOCK, dtype=jnp.int32)
    common = jnp.bitwise_and(position[:, None], position[None, :])
    parity = jnp.zeros((BLOCK, BLOCK), jnp.int32)
    for shift_bits in range(BLOCK.bit_length() - 1):
        parity = parity + jnp.bitwise_and(jnp.right_shift(common, shift_bits), 1)
    signed = 1 - 2 * jnp.bitwise_and(parity, 1)
    return signed.astype(jnp.float32) / math.sqrt(BLOCK)

def rotate(matrix, rotation):
    row_count, col_count = matrix.shape
    blocks = matrix.reshape(row_count, col_count // BLOCK, BLOCK)
    return jnp.einsum('rbk,kj->rbj', blocks, rotation, precision=lax.Precision.HIGHEST)

def reference(attn_out, out_grad, weight, sign_vector):
    input_grad = lax.dot_general(out_grad, weight, (((1,), (1,)), ((), ())), preferred_element_type=jnp.float32).astype(jnp.bfloat16)
    rotation = hadamard()
    sign_row = sign_vector.astype(jnp.float32)
    grouped_acts = attn_out.reshape(N_DP, -1, HD)
    grouped_grads = out_grad.reshape(N_DP, -1, DW)

    def rotated(operands):
        acts_group, grads_group = operands
        partial_value = lax.dot_general(acts_group, grads_group, (((0,), (0,)), ((), ())), preferred_element_type=jnp.float32)
        return rotate(partial_value * sign_row[None, :], rotation)

    def block_peak(operands):
        return lax.optimization_barrier(jnp.max(jnp.abs(rotated(operands)), axis=2))
    scale = lax.optimization_barrier(jnp.max(lax.map(block_peak, (grouped_acts, grouped_grads)), axis=0)) + EPSILON

    def accumulate(running, operands):
        turned = rotated(operands)
        quant = jnp.floor(turned * 127.0 / scale[:, :, None] + 0.5)
        return (running + quant, None)
    summed, unused = lax.scan(accumulate, jnp.zeros((HD, DW // BLOCK, BLOCK), jnp.float32), (grouped_acts, grouped_grads))
    restored = (summed * (scale[:, :, None] / 127.0)).reshape(HD, DW)
    weight_grad = rotate(restored, rotation).reshape(HD, DW) * sign_row[None, :]
    return (input_grad, weight_grad)
```

```python
import functools
import math

import jax
import jax.numpy as jnp
from jax import lax
from jax.experimental import pallas as pl
from jax.experimental.pallas import tpu as pltpu
from jax.sharding import PartitionSpec as P

BLOCK = 128
EPSILON = 1e-06
SIDE = 4
TOK = 256
SHARD = 192
TILE = 768
HALF = 384
FEATURES = 3072
MESH = pl.DeviceIdType.MESH


def hadamard_signs():
    row = lax.broadcasted_iota(jnp.int32, (BLOCK, BLOCK), 0)
    col = lax.broadcasted_iota(jnp.int32, (BLOCK, BLOCK), 1)
    common = jnp.bitwise_and(row, col)
    parity = jnp.zeros((BLOCK, BLOCK), jnp.int32)
    for shift in range(BLOCK.bit_length() - 1):
        parity = parity + jnp.bitwise_and(jnp.right_shift(common, shift), 1)
    signed = 1 - 2 * jnp.bitwise_and(parity, 1)
    return signed.astype(jnp.float32).astype(jnp.bfloat16)


def rotate(value, had):
    high = value.astype(jnp.bfloat16)
    rest = value - high.astype(jnp.float32)
    middle = rest.astype(jnp.bfloat16)
    low = (rest - middle.astype(jnp.float32)).astype(jnp.bfloat16)
    total = jnp.dot(low, had, preferred_element_type=jnp.float32)
    total = total + jnp.dot(middle, had, preferred_element_type=jnp.float32)
    total = total + jnp.dot(high, had, preferred_element_type=jnp.float32)
    return total * (1.0 / math.sqrt(BLOCK))


def kernel(
    a_ref, g_ref, w_ref, sign_ref, ig_ref, wg_ref,
    attn, grad, wbuf, g_own, ig_acc, acc, had_ref, maxima, quant, sib_in, summed, pieces, peaks, scale, scale_t,
    local_sem, a_s, a_r, g_s, g_r, w_s, w_r, h_s, h_r, m_s, m_r, q_s, q_r, p_s, p_r, c_s, c_r,
):
    dp, fsdp = lax.axis_index("dp"), lax.axis_index("fsdp")
    y, c = dp // 2, lax.rem(dp, 2)
    z, x = fsdp // SIDE, lax.rem(fsdp, SIDE)
    s = 1 - 2 * c
    off = [0, -s, s, 2]

    def mod(v):
        return lax.rem(v + 2 * SIDE, SIDE)

    def device(dx=0, dy=0, dz=0, dc=0):
        return (2 * mod(y + dy) + lax.rem(c + dc, 2), SIDE * mod(z + dz) + mod(x + dx))

    def remote(src, dst, send, recv, target):
        copy = pltpu.make_async_remote_copy(
            src_ref=src, dst_ref=dst, send_sem=send, recv_sem=recv, device_id=target, device_id_type=MESH
        )
        return copy

    sent = []

    def push(*args):
        copy = remote(*args)
        copy.start()
        sent.append(copy)
        return copy

    barrier = pltpu.get_barrier_semaphore()
    greeted = [device(dx=d) for d in range(1, SIDE)] + [device(dz=d) for d in range(1, SIDE)]
    greeted += [(lax.rem(dp + d, 8), fsdp) for d in range(1, 8)]
    for target in greeted:
        pl.semaphore_signal(barrier, inc=1, device_id=target, device_id_type=MESH)
    diagonal = x == y
    for k in range(SIDE):

        @pl.when(jnp.logical_not(jnp.logical_and(diagonal, k == y)))
        def _():
            pl.semaphore_signal(barrier, inc=1, device_id=(2 * k + c, SIDE * z + y), device_id_type=MESH)

    pl.semaphore_wait(barrier, len(greeted) + SIDE - diagonal.astype(jnp.int32))

    def shard_of(pa, pb):
        on_z = lax.select(c == 1, mod(z + off[pa]), mod(z + off[pb]))
        on_x = lax.select(c == 1, mod(x + off[pb]), mod(x + off[pa]))
        return SIDE * on_z + on_x

    def part_of(py, core=c):
        return 2 * mod(y + off[py]) + core

    def w_chunk(pa, pb, py):
        return wbuf.at[
            pl.ds(pl.multiple_of(SHARD * shard_of(pa, pb), SHARD), SHARD),
            pl.ds(pl.multiple_of(HALF * part_of(py), HALF), HALF),
        ]

    def along_a(d):
        return device(dx=lax.select(c == 1, 0, d), dz=lax.select(c == 1, d, 0))

    def along_b(d):
        return device(dx=lax.select(c == 1, d, 0), dz=lax.select(c == 1, 0, d))

    w_copies = {}

    def w_push(src, pa, pb, py, landing, target):
        ta, tb, ty = landing
        index = 16 * ty + 4 * tb + ta
        w_copies[landing] = push(src, w_chunk(pa, pb, py), w_s.at[index], w_r.at[index], target)

    w_own = w_ref.at[:, pl.ds(pl.multiple_of(HALF * dp, HALF), HALF)]
    w_push(w_own, 0, 0, 0, (1, 0, 0), along_a(s))
    w_push(w_own, 0, 0, 0, (2, 0, 0), along_a(-s))
    w_push(w_own, 0, 0, 0, (0, 1, 0), along_b(s))
    w_push(w_own, 0, 0, 0, (0, 2, 0), along_b(-s))

    def a_block(jx, kz):
        return attn.at[jx, pl.ds(TOK * kz, TOK)]

    def g_block(jx, kz):
        return grad.at[jx, pl.ds(TOK * kz, TOK)]

    def a_columns(owner):
        return a_ref.at[:, pl.ds(pl.multiple_of(TILE * owner, TILE), TILE)]

    def g_columns(owner):
        return g_ref.at[:, pl.ds(pl.multiple_of(TILE * owner, TILE), TILE)]

    a_copies, g_copies = {}, {}

    def a_push(src, landing, target):
        index = 4 * landing[0] + landing[1]
        a_copies[landing] = push(src, a_block(*landing), a_s.at[index], a_r.at[index], target)

    def g_push(src, landing, target):
        index = 4 * landing[0] + landing[1]
        g_copies[landing] = push(src, g_block(*landing), g_s.at[index], g_r.at[index], target)

    local = [
        pltpu.make_async_copy(a_columns(z), a_block(0, 0), local_sem.at[0]),
        pltpu.make_async_copy(g_columns(x), g_block(0, 0), local_sem.at[1]),
        pltpu.make_async_copy(g_ref, g_own, local_sem.at[2]),
    ]
    for py in range(SIDE):
        columns = pl.ds(pl.multiple_of(HALF * part_of(py), HALF), HALF)
        local.append(pltpu.make_async_copy(w_ref.at[:, columns], w_chunk(0, 0, py), local_sem.at[3 + py]))
    for copy in local:
        copy.start()
    for position, d in ((1, s), (2, -s), (3, 2)):
        a_push(a_columns(mod(z + d)), (0, position), device(dz=d))
        g_push(g_columns(mod(x + d)), (position, 0), device(dx=d))

    def a_spread(kz):
        a_push(a_block(0, kz), (1, kz), device(dx=s))
        a_push(a_block(0, kz), (2, kz), device(dx=-s))

    def g_spread(jx):
        g_push(g_block(jx, 0), (jx, 1), device(dz=s))
        g_push(g_block(jx, 0), (jx, 2), device(dz=-s))

    def w_spread_b(pa):
        w_push(w_chunk(pa, 0, 0), pa, 0, 0, (pa, 1, 0), along_b(s))
        w_push(w_chunk(pa, 0, 0), pa, 0, 0, (pa, 2, 0), along_b(-s))

    def w_spread_y(pa, pb):
        w_push(w_chunk(pa, pb, 0), pa, pb, 0, (pa, pb, 1), device(dy=s))
        w_push(w_chunk(pa, pb, 0), pa, pb, 0, (pa, pb, 2), device(dy=-s))

    def w_plane(pa, pb):
        w_copies[pa, pb, 0].wait_recv()
        if pb == 0:
            if pa == 1:
                w_push(w_chunk(1, 0, 0), 1, 0, 0, (3, 0, 0), along_a(s))
            w_spread_b(pa)
        if pb == 1:
            w_push(w_chunk(pa, 1, 0), pa, 1, 0, (pa, 3, 0), along_b(s))
        w_spread_y(pa, pb)

    def w_forward(pa, pb):
        w_copies[pa, pb, 1].wait_recv()
        w_push(w_chunk(pa, pb, 1), pa, pb, 1, (pa, pb, 3), device(dy=s))

    def share_copy(py, landing):
        columns = wbuf.at[:, pl.ds(pl.multiple_of(HALF * part_of(py), HALF), HALF)]
        return remote(columns, columns, h_s.at[py], h_r.at[landing], device(dc=1))

    def w_share(py):
        copy = share_copy(py, (0, 2, 1, 3)[py])
        copy.start()
        sent.append(copy)

    local[0].wait()
    a_spread(0)
    local[1].wait()
    g_spread(0)

    order = [
        (1, 0), (2, 0), (0, 1), (0, 2), (3, 0), (1, 1), (1, 2), (2, 1), (2, 2), (0, 3), (3, 1), (3, 2), (1, 3), (2, 3), (3, 3)
    ]
    for chunk in order[:4]:
        w_plane(*chunk)
    for position in (1, 2):
        a_copies[0, position].wait_recv()
        a_spread(position)
        g_copies[position, 0].wait_recv()
        g_spread(position)
    for chunk in order[4:9]:
        w_plane(*chunk)
    a_copies[0, 3].wait_recv()
    a_spread(3)
    g_copies[3, 0].wait_recv()
    g_spread(3)
    for chunk in order[:3]:
        w_forward(*chunk)
    for chunk in order[9:]:
        w_plane(*chunk)
    for copy in local[2:]:
        copy.wait()
    w_share(0)
    had_ref[...] = hadamard_signs()

    for i in range(SIDE):
        a_copies[1, i].wait_recv()
        a_push(a_block(1, i), (3, i), device(dx=s))
        g_copies[i, 1].wait_recv()
        g_push(g_block(i, 1), (i, 3), device(dz=s))
        for chunk in order[3 + 3 * i : 6 + 3 * i]:
            w_forward(*chunk)
    w_share(1)

    def partial_step(jx, low, high, first=False):
        def tile(m, carry):
            rows = pl.ds(pl.multiple_of(256 * m, 256), 256)
            value = lax.dot_general(
                attn[jx, TOK * low : TOK * high, rows],
                grad[jx, TOK * low : TOK * high, :],
                (((0,), (0,)), ((), ())),
                preferred_element_type=jnp.float32,
            )
            if first:
                acc[rows, :] = value
            else:
                acc[rows, :] += value
            return carry

        lax.fori_loop(0, TILE // 256, tile, 0)

    def input_step(py):
        share_copy(py, py).wait_recv()
        columns = pl.ds(pl.multiple_of(TILE * mod(y + off[py]), TILE), TILE)

        def tile(n, carry):
            rows = pl.ds(pl.multiple_of(512 * n, 512), 512)
            value = lax.dot_general(
                g_own[:, columns], wbuf[rows, columns], (((1,), (1,)), ((), ())), preferred_element_type=jnp.float32
            )
            if py == 0:
                ig_acc[:, rows] = value
            elif py < SIDE - 1:
                ig_acc[:, rows] += value
            else:
                ig_ref[:, rows] = (ig_acc[:, rows] + value).astype(ig_ref.dtype)
            return carry

        lax.fori_loop(0, FEATURES // 512, tile, 0)

    input_step(0)
    for i in range(SIDE):
        a_copies[2, i].wait_recv()
        g_copies[i, 2].wait_recv()
    for jx in range(3):
        partial_step(jx, 0, 3, first=jx == 0)
    for chunk in order:
        w_copies[chunk + (2,)].wait_recv()
    w_share(2)
    input_step(1)
    for i in range(SIDE):
        a_copies[3, i].wait_recv()
        g_copies[i, 3].wait_recv()
        if i < 3:
            partial_step(i, 3, 4)
    partial_step(3, 0, 4)

    maxima[...] = jnp.zeros_like(maxima)

    def turn(step, carry):
        b, m = step // 3, lax.rem(step, 3)
        rows = pl.ds(pl.multiple_of(256 * m, 256), 256)
        columns = pl.ds(pl.multiple_of(BLOCK * b, BLOCK), BLOCK)
        signs = sign_ref[:, pl.ds(pl.multiple_of(TILE * x + BLOCK * b, BLOCK), BLOCK)]
        turned = rotate(acc[rows, columns] * signs, had_ref[...])
        acc[rows, columns] = turned
        peak = jnp.max(jnp.abs(turned), axis=1, keepdims=True)
        lane = lax.broadcasted_iota(jnp.int32, (256, BLOCK), 1)
        maxima[rows, :] = jnp.where(lane == b, peak, maxima[rows, :])
        return carry

    lax.fori_loop(0, 18, turn, 0)
    for r in range(TILE // BLOCK):
        span = slice(BLOCK * r, BLOCK * r + BLOCK)
        peaks[0, :, span] = jnp.transpose(maxima[span, :])[:8]
    met = [
        push(peaks.at[0], peaks.at[d], m_s.at[d], m_r.at[d], (lax.rem(dp + d, 8), fsdp)) for d in range(1, 8)
    ]

    for chunk in order:
        w_copies[chunk + (3,)].wait_recv()
    w_share(3)

    for copy in met:
        copy.wait_recv()
    top = peaks[0]
    for d in range(1, 8):
        top = jnp.maximum(top, peaks[d])
    scale[0] = top + EPSILON
    for r in range(TILE // BLOCK):
        span = slice(BLOCK * r, BLOCK * r + BLOCK)
        scale_t[span, :] = jnp.transpose(
            jnp.concatenate([scale[0, :, span], jnp.ones((BLOCK - 8, BLOCK), jnp.float32)], axis=0)
        )

    for d in range(1, SIDE):

        @pl.when(diagonal)
        def _():
            remote(scale.at[0], scale.at[1], c_s.at[d], c_r.at[0], device(dx=d)).start()

    for b in range(TILE // BLOCK):
        columns = slice(BLOCK * b, BLOCK * b + BLOCK)

        def round_rows(m, carry):
            rows = pl.ds(pl.multiple_of(256 * m, 256), 256)
            factor = 127.0 / scale_t[rows, b : b + 1]
            quant[rows, columns] = jnp.floor(acc[rows, columns] * factor + 0.5).astype(quant.dtype)
            return carry

        lax.fori_loop(0, 3, round_rows, 0)

    mine = pl.ds(pl.multiple_of(HALF * c, HALF), HALF)
    other = pl.ds(pl.multiple_of(HALF * (1 - c), HALF), HALF)
    traded = push(quant.at[:, other], sib_in, q_s.at[0], q_r.at[0], device(dc=1))
    input_step(2)
    traded.wait_recv()
    summed[...] = quant[:, mine] + sib_in[...]

    def piece_copies(k):
        src = summed.at[pl.ds(SHARD * k, SHARD), :]
        here = pltpu.make_async_copy(src, pieces.at[y], p_s.at[k])
        away = remote(src, pieces.at[y], p_s.at[k], p_r.at[y], (2 * x + c, SIDE * z + k))
        return jnp.logical_and(diagonal, k == x), here, away

    for k in range(SIDE):
        stays, here, away = piece_copies(k)
        pl.when(stays)(here.start)
        pl.when(jnp.logical_not(stays))(away.start)

    input_step(3)

    for k in range(SIDE):
        stays, here, away = piece_copies(k)
        pl.when(stays)(here.wait)
        pl.when(jnp.logical_not(stays))(away.wait_send)
    for k in range(SIDE):
        arrives = remote(pieces.at[k], pieces.at[k], p_s.at[k], p_r.at[k], device(dx=1))
        pl.when(jnp.logical_not(jnp.logical_and(diagonal, k == y)))(arrives.wait_recv)

    @pl.when(jnp.logical_not(diagonal))
    def _():
        remote(scale.at[0], scale.at[1], c_s.at[0], c_r.at[0], device(dx=1)).wait_recv()

    @pl.when(diagonal)
    def _():
        scale[1] = scale[0]
        for d in range(1, SIDE):
            remote(scale.at[0], scale.at[1], c_s.at[d], c_r.at[0], device(dx=d)).wait_send()

    for r in range(TILE // BLOCK):
        span = slice(BLOCK * r, BLOCK * r + BLOCK)
        scale_t[span, :] = jnp.transpose(
            jnp.concatenate([scale[1, :, span], jnp.ones((BLOCK - 8, BLOCK), jnp.float32)], axis=0)
        )
    rows = pl.ds(pl.multiple_of(SHARD * x, SHARD), SHARD)
    factors = scale_t[rows, :] / 127.0
    for j in range(HALF // BLOCK):
        columns = slice(BLOCK * j, BLOCK * j + BLOCK)
        total = pieces[0, :, columns].astype(jnp.float32)
        for k in range(1, SIDE):
            total = total + pieces[k, :, columns].astype(jnp.float32)
        factor = jnp.where(c == 0, factors[:, j : j + 1], factors[:, 3 + j : 4 + j])
        signs = sign_ref[:, pl.ds(pl.multiple_of(HALF * dp + BLOCK * j, BLOCK), BLOCK)]
        wg_ref[:, columns] = rotate(total * factor, had_ref[...]) * signs

    for copy in sent:
        copy.wait_send()


def body(attn_out, out_grad, weight, sign_vector):
    signs = sign_vector.astype(jnp.float32)[None, :]
    hbm = pl.BlockSpec(memory_space=pl.ANY)
    vmem = pl.BlockSpec(memory_space=pltpu.VMEM)
    dma = pltpu.SemaphoreType.DMA
    return pl.pallas_call(
        kernel,
        out_shape=(
            jax.ShapeDtypeStruct((TOK, FEATURES), jnp.bfloat16),
            jax.ShapeDtypeStruct((SHARD, HALF), jnp.float32),
        ),
        in_specs=[hbm, hbm, hbm, vmem],
        out_specs=(vmem, vmem),
        scratch_shapes=[
            pltpu.VMEM((SIDE, SIDE * TOK, TILE), jnp.bfloat16),
            pltpu.VMEM((SIDE, SIDE * TOK, TILE), jnp.bfloat16),
            pltpu.VMEM((FEATURES, FEATURES), jnp.bfloat16),
            pltpu.VMEM((TOK, FEATURES), jnp.bfloat16),
            pltpu.VMEM((TOK, FEATURES), jnp.float32),
            pltpu.VMEM((TILE, TILE), jnp.float32),
            pltpu.VMEM((BLOCK, BLOCK), jnp.bfloat16),
            pltpu.VMEM((TILE, BLOCK), jnp.float32),
            pltpu.VMEM((TILE, TILE), jnp.bfloat16),
            pltpu.VMEM((TILE, HALF), jnp.bfloat16),
            pltpu.VMEM((TILE, HALF), jnp.bfloat16),
            pltpu.VMEM((SIDE, SHARD, HALF), jnp.bfloat16),
            pltpu.VMEM((8, 8, TILE), jnp.float32),
            pltpu.VMEM((2, 8, TILE), jnp.float32),
            pltpu.VMEM((TILE, BLOCK), jnp.float32),
            dma((8,)), dma((16,)), dma((16,)), dma((16,)), dma((16,)), dma((64,)), dma((64,)), dma((4,)), dma((4,)),
            dma((8,)), dma((8,)), dma((1,)), dma((1,)), dma((4,)), dma((4,)), dma((4,)), dma((1,)),
        ],
        compiler_params=pltpu.CompilerParams(
            collective_id=0, has_side_effects=True, vmem_limit_bytes=60 * 2**20
        ),
    )(attn_out, out_grad, weight, signs)


def solution(mesh):
    in_specs = (P(("dp", "fsdp"), None), P(("dp", "fsdp"), None), P("fsdp", None), P())
    out_specs = (P(("dp", "fsdp"), None), P("fsdp", "dp"))
    return jax.shard_map(body, mesh=mesh, in_specs=in_specs, out_specs=out_specs, check_vma=False)
```

```python
import functools
import math

import jax
import jax.numpy as jnp
from jax import lax
from jax.experimental import pallas as pl
from jax.experimental.pallas import tpu as pltpu
from jax.sharding import PartitionSpec as P

BLOCK = 128
EPSILON = 1e-06
SIDE = 4
TOK = 256
SHARD = 192
TILE = 768
QUARTER = 48
HALF = 384
FEATURES = 3072
MESH = pl.DeviceIdType.MESH


def hadamard_signs():
    row = lax.broadcasted_iota(jnp.int32, (BLOCK, BLOCK), 0)
    col = lax.broadcasted_iota(jnp.int32, (BLOCK, BLOCK), 1)
    common = jnp.bitwise_and(row, col)
    parity = jnp.zeros((BLOCK, BLOCK), jnp.int32)
    for shift in range(BLOCK.bit_length() - 1):
        parity = parity + jnp.bitwise_and(jnp.right_shift(common, shift), 1)
    signed = 1 - 2 * jnp.bitwise_and(parity, 1)
    return signed.astype(jnp.float32).astype(jnp.bfloat16)


def rotate(value, had):
    high = value.astype(jnp.bfloat16)
    rest = value - high.astype(jnp.float32)
    middle = rest.astype(jnp.bfloat16)
    low = (rest - middle.astype(jnp.float32)).astype(jnp.bfloat16)
    total = jnp.dot(low, had, preferred_element_type=jnp.float32)
    total = total + jnp.dot(middle, had, preferred_element_type=jnp.float32)
    total = total + jnp.dot(high, had, preferred_element_type=jnp.float32)
    return total * (1.0 / math.sqrt(BLOCK))


def kernel(
    a_ref, g_ref, w_ref, sign_ref, ig_ref, wg_ref,
    attn, grad, wq, others, staged, turned_ig, ig_v, acc, had_ref, eye, maxima, leaving, sib_in, summed, pieces, peaks, scale,
    scale_t, local_sem, a_s, a_r, g_s, g_r, w_s, w_r, h_s, h_r, o_s, o_r, i_s, i_r, m_s, m_r, q_s, q_r, p_s, p_r, c_s, c_r,
):
    dp, fsdp = lax.axis_index("dp"), lax.axis_index("fsdp")
    y, c = dp // 2, lax.rem(dp, 2)
    z, x = fsdp // SIDE, lax.rem(fsdp, SIDE)
    s = 1 - 2 * c
    off = [0, -s, s, 2]

    def mod(v):
        return lax.rem(v + 2 * SIDE, SIDE)

    def device(dx=0, dy=0, dz=0, dc=0):
        return (2 * mod(y + dy) + lax.rem(c + dc, 2), SIDE * mod(z + dz) + mod(x + dx))

    def remote(src, dst, send, recv, target):
        copy = pltpu.make_async_remote_copy(
            src_ref=src, dst_ref=dst, send_sem=send, recv_sem=recv, device_id=target, device_id_type=MESH
        )
        return copy

    sent = []

    def push(*args):
        copy = remote(*args)
        copy.start()
        sent.append(copy)
        return copy

    barrier = pltpu.get_barrier_semaphore()
    greeted = [device(dx=d) for d in range(1, SIDE)] + [device(dz=d) for d in range(1, SIDE)]
    greeted += [(lax.rem(dp + d, 8), fsdp) for d in range(1, 8)]
    for target in greeted:
        pl.semaphore_signal(barrier, inc=1, device_id=target, device_id_type=MESH)
    diagonal = x == y
    for k in range(SIDE):

        @pl.when(jnp.logical_not(jnp.logical_and(diagonal, k == y)))
        def _():
            pl.semaphore_signal(barrier, inc=1, device_id=(2 * k + c, SIDE * z + y), device_id_type=MESH)

    pl.semaphore_wait(barrier, len(greeted) + SIDE - diagonal.astype(jnp.int32))

    depth = FEATURES // 2
    k_half = pl.ds(pl.multiple_of(depth * c, depth), depth)
    y_rows = pl.ds(pl.multiple_of(QUARTER * y, QUARTER), QUARTER)

    def w_chunk(pa, pb):
        on_z = lax.select(c == 1, mod(z + off[pa]), mod(z + off[pb]))
        on_x = lax.select(c == 1, mod(x + off[pb]), mod(x + off[pa]))
        return wq.at[pl.ds(pl.multiple_of(QUARTER * (SIDE * on_z + on_x), QUARTER), QUARTER), k_half]

    def along_a(d):
        return device(dx=lax.select(c == 1, 0, d), dz=lax.select(c == 1, d, 0))

    def along_b(d):
        return device(dx=lax.select(c == 1, d, 0), dz=lax.select(c == 1, 0, d))

    w_copies = {}

    def w_push(src, dst, landing, target):
        index = 4 * landing[1] + landing[0]
        w_copies[landing] = push(src, dst, w_s.at[index], w_r.at[index], target)

    w_own = w_ref.at[y_rows, k_half]
    w_push(w_own, w_chunk(0, 0), (1, 0), along_a(s))
    w_push(w_own, w_chunk(0, 0), (2, 0), along_a(-s))
    w_push(w_own, w_chunk(0, 0), (3, 0), along_a(2))
    w_push(w_own, w_chunk(0, 0), (0, 1), along_b(s))
    w_push(w_own, w_chunk(0, 0), (0, 2), along_b(-s))
    w_push(w_own, w_chunk(0, 0), (0, 3), along_b(2))

    o_copies = [
        None,
        push(g_ref, others.at[1], o_s.at[0], o_r.at[0], device(dy=s)),
        push(g_ref, others.at[2], o_s.at[1], o_r.at[1], device(dy=-s)),
    ]

    def a_block(jx, kz):
        return attn.at[jx, pl.ds(TOK * kz, TOK)]

    def g_block(jx, kz):
        return grad.at[jx, pl.ds(TOK * kz, TOK)]

    def a_columns(owner):
        return a_ref.at[:, pl.ds(pl.multiple_of(TILE * owner, TILE), TILE)]

    def g_columns(owner):
        return g_ref.at[:, pl.ds(pl.multiple_of(TILE * owner, TILE), TILE)]

    a_copies, g_copies = {}, {}

    def a_push(src, landing, target):
        index = 4 * landing[0] + landing[1]
        a_copies[landing] = push(src, a_block(*landing), a_s.at[index], a_r.at[index], target)

    def g_push(src, landing, target):
        index = 4 * landing[0] + landing[1]
        g_copies[landing] = push(src, g_block(*landing), g_s.at[index], g_r.at[index], target)

    local = [
        pltpu.make_async_copy(a_columns(z), a_block(0, 0), local_sem.at[0]),
        pltpu.make_async_copy(g_columns(x), g_block(0, 0), local_sem.at[1]),
        pltpu.make_async_copy(g_ref, others.at[0], local_sem.at[2]),
        pltpu.make_async_copy(
            w_ref.at[y_rows, :],
            wq.at[pl.ds(pl.multiple_of(QUARTER * fsdp, QUARTER), QUARTER), :],
            local_sem.at[3],
        ),
    ]
    for copy in local:
        copy.start()
    for position, d in ((1, s), (2, -s), (3, 2)):
        a_push(a_columns(mod(z + d)), (0, position), device(dz=d))
        g_push(g_columns(mod(x + d)), (position, 0), device(dx=d))

    def a_spread(kz):
        a_push(a_block(0, kz), (1, kz), device(dx=s))
        a_push(a_block(0, kz), (2, kz), device(dx=-s))

    def g_spread(jx):
        g_push(g_block(jx, 0), (jx, 1), device(dz=s))
        g_push(g_block(jx, 0), (jx, 2), device(dz=-s))

    had_ref[...] = hadamard_signs()
    row = lax.broadcasted_iota(jnp.int32, (TOK, TOK), 0)
    col = lax.broadcasted_iota(jnp.int32, (TOK, TOK), 1)
    eye[...] = jnp.where(row == col, 1.0, 0.0).astype(eye.dtype)

    def own_blocks():
        local[0].wait()
        a_spread(0)
        local[1].wait()
        g_spread(0)

    def blocks(position):
        a_copies[0, position].wait_recv()
        a_spread(position)
        g_copies[position, 0].wait_recv()
        g_spread(position)

    shares = []

    def weight(pa, pb):
        w_copies[pa, pb].wait_recv()
        chunk = w_chunk(pa, pb)
        index = 4 * pb + pa
        shares.append(push(chunk, chunk, h_s.at[index], h_r.at[index], device(dc=1)))
        if pb == 0:
            w_push(chunk, chunk, (pa, 1), along_b(s))
            w_push(chunk, chunk, (pa, 2), along_b(-s))
            w_push(chunk, chunk, (pa, 3), along_b(2))

    def shared():
        local[2].wait()
        local[3].wait()
        for copy in shares:
            copy.wait_recv()

    def forward(i):
        a_copies[1, i].wait_recv()
        a_push(a_block(1, i), (3, i), device(dx=s))
        g_copies[i, 1].wait_recv()
        g_push(g_block(i, 1), (i, 3), device(dz=s))

    def pass_on():
        o_copies[1].wait_recv()
        o_copies.append(push(others.at[1], others.at[3], o_s.at[2], o_r.at[2], device(dy=s)))

    def partial_step(jx, low, high, first=False):
        def tile(m, carry):
            rows = pl.ds(pl.multiple_of(256 * m, 256), 256)
            value = lax.dot_general(
                attn[jx, TOK * low : TOK * high, rows],
                grad[jx, TOK * low : TOK * high, :],
                (((0,), (0,)), ((), ())),
                preferred_element_type=jnp.float32,
            )
            if first:
                acc[rows, :] = value
            else:
                acc[rows, :] += value
            return carry

        lax.fori_loop(0, TILE // 256, tile, 0)

    i_copies = []

    def slab(slot):
        if slot > 1:
            o_copies[slot].wait_recv()

        def tile(n, carry):
            rows = pl.ds(pl.multiple_of(HALF * n, HALF), HALF)
            shards = pl.ds(8 * n, 8)
            value = lax.dot_general(
                wq[rows, :], others[slot], (((1,), (1,)), ((), ())), preferred_element_type=jnp.float32
            )
            value = value.astype(staged.dtype).reshape(8, QUARTER, TOK)
            if slot == 0:
                turned_ig[shards, y_rows, :] = value
            else:
                staged[slot - 1, shards] = value
            return carry

        lax.fori_loop(0, TILE // HALF, tile, 0)
        if slot:
            landing = turned_ig.at[:, y_rows, :]
            i_copies.append(
                push(staged.at[slot - 1], landing, i_s.at[slot - 1], i_r.at[slot - 1], device(dy=off[slot]))
            )

    def write_input_grad():
        for copy in i_copies:
            copy.wait_recv()

        def tile(n, carry):
            value = lax.dot_general(
                eye[...],
                turned_ig[pl.ds(2 * n, 2)].reshape(HALF, TOK),
                (((1,), (1,)), ((), ())),
                preferred_element_type=jnp.float32,
            )
            ig_v[:, pl.ds(pl.multiple_of(HALF * n, HALF), HALF)] = value.astype(ig_v.dtype)
            return carry

        lax.fori_loop(0, FEATURES // HALF, tile, 0)
        ig_out.start()

    ig_out = pltpu.make_async_copy(ig_v, ig_ref, local_sem.at[4])

    weight(1, 0)
    weight(2, 0)
    weight(3, 0)
    own_blocks()
    weight(0, 1)
    weight(0, 2)
    weight(1, 1)
    weight(1, 2)
    weight(2, 1)
    weight(2, 2)
    weight(0, 3)
    weight(3, 1)
    weight(3, 2)
    weight(1, 3)
    weight(2, 3)
    weight(3, 3)
    blocks(1)
    blocks(2)
    blocks(3)
    pass_on()
    shared()
    slab(0)
    slab(1)
    slab(2)
    forward(0)
    forward(1)
    slab(3)
    forward(2)
    forward(3)
    partial_step(0, 0, 2, first=True)
    partial_step(1, 0, 2)

    for i in range(SIDE):
        a_copies[2, i].wait_recv()
        g_copies[i, 2].wait_recv()
    partial_step(0, 2, 3)
    partial_step(1, 2, 3)
    partial_step(2, 0, 3)
    for i in range(SIDE):
        a_copies[3, i].wait_recv()
        g_copies[i, 3].wait_recv()
        if i < 3:
            partial_step(i, 3, 4)
        partial_step(3, i, i + 1)

    maxima[...] = jnp.zeros_like(maxima)

    def turn(step, carry):
        b, m = step // 3, lax.rem(step, 3)
        rows = pl.ds(pl.multiple_of(256 * m, 256), 256)
        columns = pl.ds(pl.multiple_of(BLOCK * b, BLOCK), BLOCK)
        signs = sign_ref[:, pl.ds(pl.multiple_of(TILE * x + BLOCK * b, BLOCK), BLOCK)].astype(jnp.float32)
        turned = rotate(acc[rows, columns] * signs, had_ref[...])
        acc[rows, columns] = turned
        peak = jnp.max(jnp.abs(turned), axis=1, keepdims=True)
        lane = lax.broadcasted_iota(jnp.int32, (256, BLOCK), 1)
        maxima[rows, :] = jnp.where(lane == b, peak, maxima[rows, :])
        return carry

    lax.fori_loop(0, 18, turn, 0)
    for r in range(TILE // BLOCK):
        span = slice(BLOCK * r, BLOCK * r + BLOCK)
        peaks[0, :, span] = jnp.transpose(maxima[span, :])[:8]
    met = [
        push(peaks.at[0], peaks.at[d], m_s.at[d], m_r.at[d], (lax.rem(dp + d, 8), fsdp)) for d in range(1, 8)
    ]
    write_input_grad()
    for copy in met:
        copy.wait_recv()
    top = peaks[0]
    for d in range(1, 8):
        top = jnp.maximum(top, peaks[d])
    scale[0] = top + EPSILON

    for d in range(1, SIDE):

        @pl.when(diagonal)
        def _():
            remote(scale.at[0], scale.at[1], c_s.at[d], c_r.at[0], device(dx=d)).start()

    for r in range(TILE // BLOCK):
        span = slice(BLOCK * r, BLOCK * r + BLOCK)
        scale_t[span, :] = jnp.transpose(
            jnp.concatenate([127.0 / scale[0, :, span], jnp.ones((BLOCK - 8, BLOCK), jnp.float32)], axis=0)
        )

    def quantize(target, side, k):
        rows = slice(SHARD * k, SHARD * k + SHARD)
        for j in range(HALF // BLOCK):
            source = pl.ds(pl.multiple_of(HALF * side + BLOCK * j, BLOCK), BLOCK)
            factor = jnp.where(side == 0, scale_t[rows, j : j + 1], scale_t[rows, 3 + j : 4 + j])
            target[rows, BLOCK * j : BLOCK * j + BLOCK] = jnp.floor(acc[rows, source] * factor + 0.5).astype(target.dtype)

    traded = []
    for k in range(SIDE):
        quantize(leaving, 1 - c, k)
        span = pl.ds(SHARD * k, SHARD)
        traded.append(push(leaving.at[span, :], sib_in.at[span, :], q_s.at[k], q_r.at[k], device(dc=1)))

    def piece_copies(k):
        src = summed.at[pl.ds(SHARD * k, SHARD), :]
        here = pltpu.make_async_copy(src, pieces.at[y], p_s.at[k])
        away = remote(src, pieces.at[y], p_s.at[k], p_r.at[y], (2 * x + c, SIDE * z + k))
        return jnp.logical_and(diagonal, k == x), here, away

    for k in range(SIDE):
        quantize(summed, c, k)
        traded[k].wait_recv()
        span = slice(SHARD * k, SHARD * k + SHARD)
        summed[span, :] += sib_in[span, :]
        stays, here, away = piece_copies(k)
        pl.when(stays)(here.start)
        pl.when(jnp.logical_not(stays))(away.start)

    @pl.when(jnp.logical_not(diagonal))
    def _():
        remote(scale.at[0], scale.at[1], c_s.at[0], c_r.at[0], device(dx=1)).wait_recv()

    @pl.when(diagonal)
    def _():
        scale[1] = scale[0]
        for d in range(1, SIDE):
            remote(scale.at[0], scale.at[1], c_s.at[d], c_r.at[0], device(dx=d)).wait_send()

    for r in range(TILE // BLOCK):
        span = slice(BLOCK * r, BLOCK * r + BLOCK)
        scale_t[span, :] = jnp.transpose(
            jnp.concatenate([scale[1, :, span] / 127.0, jnp.ones((BLOCK - 8, BLOCK), jnp.float32)], axis=0)
        )
    for k in range(SIDE):
        stays, here, away = piece_copies(k)
        pl.when(stays)(here.wait)
        pl.when(jnp.logical_not(stays))(away.wait_send)
    for k in range(SIDE):
        arrives = remote(pieces.at[k], pieces.at[k], p_s.at[k], p_r.at[k], device(dx=1))
        pl.when(jnp.logical_not(jnp.logical_and(diagonal, k == y)))(arrives.wait_recv)

    rows = pl.ds(pl.multiple_of(SHARD * x, SHARD), SHARD)
    factors = scale_t[rows, :]
    for j in range(HALF // BLOCK):
        columns = slice(BLOCK * j, BLOCK * j + BLOCK)
        total = pieces[0, :, columns].astype(jnp.float32)
        for k in range(1, SIDE):
            total = total + pieces[k, :, columns].astype(jnp.float32)
        factor = jnp.where(c == 0, factors[:, j : j + 1], factors[:, 3 + j : 4 + j])
        signs = sign_ref[:, pl.ds(pl.multiple_of(HALF * dp + BLOCK * j, BLOCK), BLOCK)].astype(jnp.float32)
        wg_ref[:, columns] = rotate(total * factor, had_ref[...]) * signs

    ig_out.wait()
    for copy in sent:
        copy.wait_send()


def body(attn_out, out_grad, weight, sign_vector):
    signs = sign_vector[None, :]
    hbm = pl.BlockSpec(memory_space=pl.ANY)
    vmem = pl.BlockSpec(memory_space=pltpu.VMEM)
    dma = pltpu.SemaphoreType.DMA
    return pl.pallas_call(
        kernel,
        out_shape=(
            jax.ShapeDtypeStruct((TOK, FEATURES), jnp.bfloat16),
            jax.ShapeDtypeStruct((SHARD, HALF), jnp.float32),
        ),
        in_specs=[hbm, hbm, hbm, vmem],
        out_specs=(hbm, vmem),
        scratch_shapes=[
            pltpu.VMEM((SIDE, SIDE * TOK, TILE), jnp.bfloat16),
            pltpu.VMEM((SIDE, SIDE * TOK, TILE), jnp.bfloat16),
            pltpu.VMEM((TILE, FEATURES), jnp.bfloat16),
            pltpu.VMEM((SIDE, TOK, FEATURES), jnp.bfloat16),
            pltpu.VMEM((3, 16, QUARTER, TOK), jnp.bfloat16),
            pltpu.VMEM((16, SHARD, TOK), jnp.bfloat16),
            pltpu.VMEM((TOK, FEATURES), jnp.bfloat16),
            pltpu.VMEM((TILE, TILE), jnp.float32),
            pltpu.VMEM((BLOCK, BLOCK), jnp.bfloat16),
            pltpu.VMEM((TOK, TOK), jnp.bfloat16),
            pltpu.VMEM((TILE, BLOCK), jnp.float32),
            pltpu.VMEM((TILE, HALF), jnp.bfloat16),
            pltpu.VMEM((TILE, HALF), jnp.bfloat16),
            pltpu.VMEM((TILE, HALF), jnp.bfloat16),
            pltpu.VMEM((SIDE, SHARD, HALF), jnp.bfloat16),
            pltpu.VMEM((8, 8, TILE), jnp.float32),
            pltpu.VMEM((2, 8, TILE), jnp.float32),
            pltpu.VMEM((TILE, BLOCK), jnp.float32),
            dma((5,)), dma((16,)), dma((16,)), dma((16,)), dma((16,)), dma((16,)), dma((16,)), dma((16,)), dma((16,)),
            dma((3,)), dma((3,)), dma((3,)), dma((3,)), dma((8,)), dma((8,)), dma((4,)), dma((4,)), dma((4,)), dma((4,)),
            dma((4,)), dma((1,)),
        ],
        compiler_params=pltpu.CompilerParams(
            collective_id=0, has_side_effects=True, vmem_limit_bytes=60 * 2**20
        ),
    )(attn_out, out_grad, weight, signs)


def solution(mesh):
    in_specs = (P(("dp", "fsdp"), None), P(("dp", "fsdp"), None), P("fsdp", None), P())
    out_specs = (P(("dp", "fsdp"), None), P("fsdp", "dp"))
    return jax.shard_map(body, mesh=mesh, in_specs=in_specs, out_specs=out_specs, check_vma=False)
```

```python
import functools
import math

import jax
import jax.numpy as jnp
from jax import lax
from jax.experimental import pallas as pl
from jax.experimental.pallas import tpu as pltpu
from jax.sharding import PartitionSpec as P

BLOCK = 128
EPSILON = 1e-06
SIDE = 4
TOK = 256
SHARD = 192
TILE = 768
QUARTER = 48
HALF = 384
FEATURES = 3072
MESH = pl.DeviceIdType.MESH


def hadamard_signs():
    row = lax.broadcasted_iota(jnp.int32, (2 * BLOCK, 2 * BLOCK), 0)
    col = lax.broadcasted_iota(jnp.int32, (2 * BLOCK, 2 * BLOCK), 1)
    common = jnp.bitwise_and(row, col)
    parity = jnp.zeros((2 * BLOCK, 2 * BLOCK), jnp.int32)
    for shift in range(BLOCK.bit_length() - 1):
        parity = parity + jnp.bitwise_and(jnp.right_shift(common, shift), 1)
    signed = 1 - 2 * jnp.bitwise_and(parity, 1)
    signed = jnp.where(row // BLOCK == col // BLOCK, signed, 0)
    return signed.astype(jnp.float32).astype(jnp.bfloat16)


def rotate(value, had):
    high = value.astype(jnp.bfloat16)
    rest = value - high.astype(jnp.float32)
    middle = rest.astype(jnp.bfloat16)
    low = (rest - middle.astype(jnp.float32)).astype(jnp.bfloat16)
    total = jnp.dot(low, had, preferred_element_type=jnp.float32)
    total = total + jnp.dot(middle, had, preferred_element_type=jnp.float32)
    total = total + jnp.dot(high, had, preferred_element_type=jnp.float32)
    return total * (1.0 / math.sqrt(BLOCK))


def kernel(
    a_ref, g_ref, w_ref, sign_ref, ig_ref, wg_ref,
    attn, grad, wq, others, staged, turned_ig, ig_v, acc, had_ref, eye, maxima, leaving, sib_in, summed, pieces, peaks, scale,
    scale_t, local_sem, a_s, a_r, g_s, g_r, w_s, w_r, h_s, h_r, o_s, o_r, i_s, i_r, m_s, m_r, q_s, q_r, p_s, p_r, c_s, c_r,
):
    dp, fsdp = lax.axis_index("dp"), lax.axis_index("fsdp")
    y, c = dp // 2, lax.rem(dp, 2)
    z, x = fsdp // SIDE, lax.rem(fsdp, SIDE)
    s = 1 - 2 * c
    off = [0, -s, s, 2]

    def mod(v):
        return lax.rem(v + 2 * SIDE, SIDE)

    def device(dx=0, dy=0, dz=0, dc=0):
        return (2 * mod(y + dy) + lax.rem(c + dc, 2), SIDE * mod(z + dz) + mod(x + dx))

    def remote(src, dst, send, recv, target):
        copy = pltpu.make_async_remote_copy(
            src_ref=src, dst_ref=dst, send_sem=send, recv_sem=recv, device_id=target, device_id_type=MESH
        )
        return copy

    sent = []

    def push(*args):
        copy = remote(*args)
        copy.start()
        sent.append(copy)
        return copy

    barrier = pltpu.get_barrier_semaphore()
    greeted = [device(dx=d) for d in range(1, SIDE)] + [device(dz=d) for d in range(1, SIDE)]
    greeted += [(lax.rem(dp + d, 8), fsdp) for d in range(1, 8)]
    for target in greeted:
        pl.semaphore_signal(barrier, inc=1, device_id=target, device_id_type=MESH)
    diagonal = x == y
    for k in range(SIDE):

        @pl.when(jnp.logical_not(jnp.logical_and(diagonal, k == y)))
        def _():
            pl.semaphore_signal(barrier, inc=1, device_id=(2 * k + c, SIDE * z + y), device_id_type=MESH)

    had_ref[...] = hadamard_signs()
    row = lax.broadcasted_iota(jnp.int32, (TOK, TOK), 0)
    col = lax.broadcasted_iota(jnp.int32, (TOK, TOK), 1)
    eye[...] = jnp.where(row == col, 1.0, 0.0).astype(eye.dtype)

    maxima[...] = jnp.zeros_like(maxima)
    pl.semaphore_wait(barrier, len(greeted) + SIDE - diagonal.astype(jnp.int32))

    depth = FEATURES // 2
    k_half = pl.ds(pl.multiple_of(depth * c, depth), depth)
    y_rows = pl.ds(pl.multiple_of(QUARTER * y, QUARTER), QUARTER)

    def w_chunk(pa, pb):
        on_z = lax.select(c == 1, mod(z + off[pa]), mod(z + off[pb]))
        on_x = lax.select(c == 1, mod(x + off[pb]), mod(x + off[pa]))
        return wq.at[pl.ds(pl.multiple_of(QUARTER * (SIDE * on_z + on_x), QUARTER), QUARTER), k_half]

    def along_a(d):
        return device(dx=lax.select(c == 1, 0, d), dz=lax.select(c == 1, d, 0))

    def along_b(d):
        return device(dx=lax.select(c == 1, d, 0), dz=lax.select(c == 1, 0, d))

    w_copies = {}

    def w_push(src, dst, landing, target):
        index = 4 * landing[1] + landing[0]
        w_copies[landing] = push(src, dst, w_s.at[index], w_r.at[index], target)

    w_own = w_ref.at[y_rows, k_half]
    w_push(w_own, w_chunk(0, 0), (1, 0), along_a(s))
    w_push(w_own, w_chunk(0, 0), (2, 0), along_a(-s))
    w_push(w_own, w_chunk(0, 0), (3, 0), along_a(2))
    w_push(w_own, w_chunk(0, 0), (0, 1), along_b(s))
    w_push(w_own, w_chunk(0, 0), (0, 2), along_b(-s))

    o_copies = [
        None,
        push(g_ref, others.at[1], o_s.at[0], o_r.at[0], device(dy=s)),
        push(g_ref, others.at[2], o_s.at[1], o_r.at[1], device(dy=-s)),
    ]

    def a_block(jx, kz):
        return attn.at[jx, pl.ds(TOK * kz, TOK)]

    def g_block(jx, kz):
        return grad.at[jx, pl.ds(TOK * kz, TOK)]

    def a_columns(owner):
        return a_ref.at[:, pl.ds(pl.multiple_of(TILE * owner, TILE), TILE)]

    def g_columns(owner):
        return g_ref.at[:, pl.ds(pl.multiple_of(TILE * owner, TILE), TILE)]

    a_copies, g_copies = {}, {}

    def a_push(src, landing, target):
        index = 4 * landing[0] + landing[1]
        a_copies[landing] = push(src, a_block(*landing), a_s.at[index], a_r.at[index], target)

    def g_push(src, landing, target):
        index = 4 * landing[0] + landing[1]
        g_copies[landing] = push(src, g_block(*landing), g_s.at[index], g_r.at[index], target)

    local = [
        pltpu.make_async_copy(a_columns(z), a_block(0, 0), local_sem.at[0]),
        pltpu.make_async_copy(g_columns(x), g_block(0, 0), local_sem.at[1]),
        pltpu.make_async_copy(g_ref, others.at[0], local_sem.at[2]),
        pltpu.make_async_copy(
            w_ref.at[y_rows, :],
            wq.at[pl.ds(pl.multiple_of(QUARTER * fsdp, QUARTER), QUARTER), :],
            local_sem.at[3],
        ),
    ]
    for copy in local:
        copy.start()
    for position, d in ((1, s), (2, -s), (3, 2)):
        a_push(a_columns(mod(z + d)), (0, position), device(dz=d))
        g_push(g_columns(mod(x + d)), (position, 0), device(dx=d))

    def a_spread(kz):
        a_push(a_block(0, kz), (1, kz), device(dx=s))
        a_push(a_block(0, kz), (2, kz), device(dx=-s))

    def g_spread(jx):
        g_push(g_block(jx, 0), (jx, 1), device(dz=s))
        g_push(g_block(jx, 0), (jx, 2), device(dz=-s))

    def own_blocks():
        local[0].wait()
        a_spread(0)
        local[1].wait()
        g_spread(0)

    def blocks(position):
        a_copies[0, position].wait_recv()
        a_spread(position)
        g_copies[position, 0].wait_recv()
        g_spread(position)

    shares = []

    def weight(pa, pb):
        w_copies[pa, pb].wait_recv()
        chunk = w_chunk(pa, pb)
        index = 4 * pb + pa
        shares.append(push(chunk, chunk, h_s.at[index], h_r.at[index], device(dc=1)))
        if pb == 0:
            w_push(chunk, chunk, (pa, 1), along_b(s))
            w_push(chunk, chunk, (pa, 2), along_b(-s))
            if pa in ():
                w_push(chunk, chunk, (pa, 3), along_b(2))
        if pb == 1 and pa in (0, 1, 2, 3):
            w_push(chunk, chunk, (pa, 3), along_b(s))

    def shared():
        local[2].wait()
        local[3].wait()
        for copy in shares:
            copy.wait_recv()

    def forward(i):
        a_copies[1, i].wait_recv()
        a_push(a_block(1, i), (3, i), device(dx=s))
        g_copies[i, 1].wait_recv()
        g_push(g_block(i, 1), (i, 3), device(dz=s))

    def pass_on():
        o_copies[1].wait_recv()
        o_copies.append(push(others.at[1], others.at[3], o_s.at[2], o_r.at[2], device(dy=s)))

    def partial_step(jx, low, high, first=False):
        def tile(m, carry):
            rows = pl.ds(pl.multiple_of(256 * m, 256), 256)
            value = lax.dot_general(
                attn[jx, TOK * low : TOK * high, rows],
                grad[jx, TOK * low : TOK * high, :],
                (((0,), (0,)), ((), ())),
                preferred_element_type=jnp.float32,
            )
            if first:
                acc[rows, :] = value
            else:
                acc[rows, :] += value
            return carry

        lax.fori_loop(0, TILE // 256, tile, 0)

    i_copies = []

    def slab(slot):
        if slot > 1:
            o_copies[slot].wait_recv()

        def tile(n, carry):
            rows = pl.ds(pl.multiple_of(HALF * n, HALF), HALF)
            shards = pl.ds(8 * n, 8)
            value = lax.dot_general(
                wq[rows, :], others[slot], (((1,), (1,)), ((), ())), preferred_element_type=jnp.float32
            )
            value = value.astype(staged.dtype).reshape(8, QUARTER, TOK)
            if slot == 0:
                turned_ig[shards, y_rows, :] = value
            else:
                staged[slot - 1, shards] = value
            return carry

        lax.fori_loop(0, TILE // HALF, tile, 0)
        if slot:
            landing = turned_ig.at[:, y_rows, :]
            i_copies.append(
                push(staged.at[slot - 1], landing, i_s.at[slot - 1], i_r.at[slot - 1], device(dy=off[slot]))
            )

    def write_input_grad():
        for copy in i_copies:
            copy.wait_recv()

        def tile(n, carry):
            value = lax.dot_general(
                eye[...],
                turned_ig[pl.ds(2 * n, 2)].reshape(HALF, TOK),
                (((1,), (1,)), ((), ())),
                preferred_element_type=jnp.float32,
            )
            ig_v[:, pl.ds(pl.multiple_of(HALF * n, HALF), HALF)] = value.astype(ig_v.dtype)
            return carry

        lax.fori_loop(0, FEATURES // HALF, tile, 0)
        ig_out.start()

    ig_out = pltpu.make_async_copy(ig_v, ig_ref, local_sem.at[4])

    weight(1, 0)
    weight(2, 0)
    weight(3, 0)
    weight(0, 1)
    weight(1, 1)
    weight(2, 1)
    weight(3, 1)
    own_blocks()
    weight(0, 2)
    weight(1, 2)
    weight(2, 2)
    weight(3, 2)
    pass_on()
    weight(0, 3)
    weight(1, 3)
    weight(2, 3)
    weight(3, 3)
    blocks(1)
    blocks(2)
    blocks(3)
    shared()
    slab(1)
    slab(2)
    slab(0)
    forward(0)
    forward(1)
    slab(3)
    forward(2)
    forward(3)
    partial_step(0, 0, 2, first=True)
    partial_step(1, 0, 2)

    for i in range(SIDE):
        a_copies[2, i].wait_recv()
        g_copies[i, 2].wait_recv()
    partial_step(0, 2, 3)
    partial_step(1, 2, 3)
    partial_step(2, 0, 3)
    for i in range(SIDE):
        a_copies[3, i].wait_recv()
        g_copies[i, 3].wait_recv()
        if i < 3:
            partial_step(i, 3, 4)
        partial_step(3, i, i + 1)


    def turn(pair, carry):
        columns = pl.ds(pl.multiple_of(2 * BLOCK * pair, 2 * BLOCK), 2 * BLOCK)
        signs = sign_ref[:, pl.ds(pl.multiple_of(TILE * x + 2 * BLOCK * pair, BLOCK), 2 * BLOCK)].astype(jnp.float32)
        for m in range(3):
            rows = slice(256 * m, 256 * m + 256)
            turned = rotate(acc[rows, columns] * signs, had_ref[...])
            acc[rows, columns] = turned
            size = jnp.abs(turned)
            lane = lax.broadcasted_iota(jnp.int32, (256, BLOCK), 1)
            first = jnp.max(size[:, :BLOCK], axis=1, keepdims=True)
            second = jnp.max(size[:, BLOCK:], axis=1, keepdims=True)
            found = jnp.where(lane == 2 * pair + 1, second, maxima[rows, :])
            maxima[rows, :] = jnp.where(lane == 2 * pair, first, found)
        return carry

    lax.fori_loop(0, 3, turn, 0)
    for r in range(TILE // BLOCK):
        span = slice(BLOCK * r, BLOCK * r + BLOCK)
        peaks[0, :, span] = jnp.transpose(maxima[span, :])[:8]
    met = [
        push(peaks.at[0], peaks.at[d], m_s.at[d], m_r.at[d], (lax.rem(dp + d, 8), fsdp)) for d in range(1, 8)
    ]
    for copy in met:
        copy.wait_recv()
    top = peaks[0]
    for d in range(1, 8):
        top = jnp.maximum(top, peaks[d])
    scale[0] = top + EPSILON

    for d in range(1, SIDE):

        @pl.when(diagonal)
        def _():
            remote(scale.at[0], scale.at[1], c_s.at[d], c_r.at[0], device(dx=d)).start()

    for r in range(TILE // BLOCK):
        span = slice(BLOCK * r, BLOCK * r + BLOCK)
        scale_t[span, :] = jnp.transpose(
            jnp.concatenate([127.0 / scale[0, :, span], jnp.ones((BLOCK - 8, BLOCK), jnp.float32)], axis=0)
        )

    def quantize(target, side, k):
        rows = slice(SHARD * k, SHARD * k + SHARD)
        for j in range(HALF // BLOCK):
            source = pl.ds(pl.multiple_of(HALF * side + BLOCK * j, BLOCK), BLOCK)
            factor = jnp.where(side == 0, scale_t[rows, j : j + 1], scale_t[rows, 3 + j : 4 + j])
            target[rows, BLOCK * j : BLOCK * j + BLOCK] = jnp.floor(acc[rows, source] * factor + 0.5).astype(target.dtype)

    def piece_copies(k):
        src = summed.at[pl.ds(SHARD * k, SHARD), :]
        here = pltpu.make_async_copy(src, pieces.at[y], p_s.at[k])
        away = remote(src, pieces.at[y], p_s.at[k], p_r.at[y], (2 * x + c, SIDE * z + k))
        return jnp.logical_and(diagonal, k == x), here, away

    traded = []

    def finish(k):
        traded[k].wait_recv()
        span = slice(SHARD * k, SHARD * k + SHARD)
        summed[span, :] += sib_in[span, :]
        stays, here, away = piece_copies(k)
        pl.when(stays)(here.start)
        pl.when(jnp.logical_not(stays))(away.start)

    for k in range(SIDE):
        quantize(leaving, 1 - c, k)
        span = pl.ds(SHARD * k, SHARD)
        traded.append(push(leaving.at[span, :], sib_in.at[span, :], q_s.at[k], q_r.at[k], device(dc=1)))
        quantize(summed, c, k)
        if k:
            finish(k - 1)
    finish(SIDE - 1)

    write_input_grad()
    for copy in sent:
        copy.wait_send()

    @pl.when(jnp.logical_not(diagonal))
    def _():
        remote(scale.at[0], scale.at[1], c_s.at[0], c_r.at[0], device(dx=1)).wait_recv()

    @pl.when(diagonal)
    def _():
        scale[1] = scale[0]
        for d in range(1, SIDE):
            remote(scale.at[0], scale.at[1], c_s.at[d], c_r.at[0], device(dx=d)).wait_send()

    for r in range(TILE // BLOCK):
        span = slice(BLOCK * r, BLOCK * r + BLOCK)
        scale_t[span, :] = jnp.transpose(
            jnp.concatenate([scale[1, :, span] / 127.0, jnp.ones((BLOCK - 8, BLOCK), jnp.float32)], axis=0)
        )
    for k in range(SIDE):
        stays, here, away = piece_copies(k)
        pl.when(stays)(here.wait)
        pl.when(jnp.logical_not(stays))(away.wait_send)
    for k in range(SIDE):
        arrives = remote(pieces.at[k], pieces.at[k], p_s.at[k], p_r.at[k], device(dx=1))
        pl.when(jnp.logical_not(jnp.logical_and(diagonal, k == y)))(arrives.wait_recv)

    rows = pl.ds(pl.multiple_of(SHARD * x, SHARD), SHARD)
    factors = scale_t[rows, :]
    for j in range(HALF // BLOCK):
        columns = slice(BLOCK * j, BLOCK * j + BLOCK)
        total = pieces[0, :, columns].astype(jnp.float32)
        for k in range(1, SIDE):
            total = total + pieces[k, :, columns].astype(jnp.float32)
        factor = jnp.where(c == 0, factors[:, j : j + 1], factors[:, 3 + j : 4 + j])
        signs = sign_ref[:, pl.ds(pl.multiple_of(HALF * dp + BLOCK * j, BLOCK), BLOCK)].astype(jnp.float32)
        wg_ref[:, columns] = rotate(total * factor, had_ref[:BLOCK, :BLOCK]) * signs

    ig_out.wait()


def copy_kernel(ig_ref, wg_ref, ig_out, wg_out, ig_v, wg_v, sems):
    steps = [(wg_ref, wg_v, wg_out, 0)]
    for part in range(4):
        rows = pl.ds(part * TOK // 4, TOK // 4)
        steps.append((ig_ref.at[rows], ig_v.at[rows], ig_out.at[rows], 1 + part))
    for source, held, _, index in steps:
        pltpu.make_async_copy(source, held, sems.at[index]).start()
    for source, held, target, index in steps:
        pltpu.make_async_copy(source, held, sems.at[index]).wait()
        pltpu.make_async_copy(held, target, sems.at[8 + index]).start()
    for _, held, target, index in steps:
        pltpu.make_async_copy(held, target, sems.at[8 + index]).wait()


def body(attn_out, out_grad, weight, sign_vector):
    signs = sign_vector[None, :]
    hbm = pl.BlockSpec(memory_space=pl.ANY)
    vmem = pl.BlockSpec(memory_space=pltpu.VMEM)
    dma = pltpu.SemaphoreType.DMA
    made = pl.pallas_call(
        kernel,
        out_shape=(
            jax.ShapeDtypeStruct((TOK, FEATURES), jnp.bfloat16),
            jax.ShapeDtypeStruct((SHARD, HALF), jnp.float32),
        ),
        in_specs=[hbm, hbm, hbm, vmem],
        out_specs=(hbm, vmem),
        scratch_shapes=[
            pltpu.VMEM((SIDE, SIDE * TOK, TILE), jnp.bfloat16),
            pltpu.VMEM((SIDE, SIDE * TOK, TILE), jnp.bfloat16),
            pltpu.VMEM((TILE, FEATURES), jnp.bfloat16),
            pltpu.VMEM((SIDE, TOK, FEATURES), jnp.bfloat16),
            pltpu.VMEM((3, 16, QUARTER, TOK), jnp.bfloat16),
            pltpu.VMEM((16, SHARD, TOK), jnp.bfloat16),
            pltpu.VMEM((TOK, FEATURES), jnp.bfloat16),
            pltpu.VMEM((TILE, TILE), jnp.float32),
            pltpu.VMEM((2 * BLOCK, 2 * BLOCK), jnp.bfloat16),
            pltpu.VMEM((TOK, TOK), jnp.bfloat16),
            pltpu.VMEM((TILE, BLOCK), jnp.float32),
            pltpu.VMEM((TILE, HALF), jnp.bfloat16),
            pltpu.VMEM((TILE, HALF), jnp.bfloat16),
            pltpu.VMEM((TILE, HALF), jnp.bfloat16),
            pltpu.VMEM((SIDE, SHARD, HALF), jnp.bfloat16),
            pltpu.VMEM((8, 8, TILE), jnp.float32),
            pltpu.VMEM((2, 8, TILE), jnp.float32),
            pltpu.VMEM((TILE, BLOCK), jnp.float32),
            dma((5,)), dma((16,)), dma((16,)), dma((16,)), dma((16,)), dma((16,)), dma((16,)), dma((16,)), dma((16,)),
            dma((3,)), dma((3,)), dma((3,)), dma((3,)), dma((8,)), dma((8,)), dma((4,)), dma((4,)), dma((4,)), dma((4,)),
            dma((4,)), dma((1,)),
        ],
        compiler_params=pltpu.CompilerParams(
            collective_id=0, has_side_effects=True, vmem_limit_bytes=60 * 2**20
        ),
    )(attn_out, out_grad, weight, signs)
    return pl.pallas_call(
        copy_kernel,
        out_shape=tuple(jax.ShapeDtypeStruct(part.shape, part.dtype) for part in made),
        in_specs=[hbm, hbm],
        out_specs=(hbm, hbm),
        scratch_shapes=[
            pltpu.VMEM((TOK, FEATURES), jnp.bfloat16), pltpu.VMEM((SHARD, HALF), jnp.float32), dma((16,))
        ],
    )(*made)


def solution(mesh):
    in_specs = (P(("dp", "fsdp"), None), P(("dp", "fsdp"), None), P("fsdp", None), P())
    out_specs = (P(("dp", "fsdp"), None), P("fsdp", "dp"))
    return jax.shard_map(body, mesh=mesh, in_specs=in_specs, out_specs=out_specs, check_vma=False)
```

```python
import functools
import math

import jax
import jax.numpy as jnp
from jax import lax
from jax.experimental import pallas as pl
from jax.experimental.pallas import tpu as pltpu
from jax.sharding import PartitionSpec as P

BLOCK = 128
EPSILON = 1e-06
SIDE = 4
TOK = 256
SHARD = 192
TILE = 768
QUARTER = 48
HALF = 384
FEATURES = 3072
MESH = pl.DeviceIdType.MESH


def hadamard_signs():
    row = lax.broadcasted_iota(jnp.int32, (2 * BLOCK, 2 * BLOCK), 0)
    col = lax.broadcasted_iota(jnp.int32, (2 * BLOCK, 2 * BLOCK), 1)
    common = jnp.bitwise_and(row, col)
    parity = jnp.zeros((2 * BLOCK, 2 * BLOCK), jnp.int32)
    for shift in range(BLOCK.bit_length() - 1):
        parity = parity + jnp.bitwise_and(jnp.right_shift(common, shift), 1)
    signed = 1 - 2 * jnp.bitwise_and(parity, 1)
    signed = jnp.where(row // BLOCK == col // BLOCK, signed, 0)
    return signed.astype(jnp.float32).astype(jnp.bfloat16)


def rotate(value, had):
    high = value.astype(jnp.bfloat16)
    rest = value - high.astype(jnp.float32)
    middle = rest.astype(jnp.bfloat16)
    low = (rest - middle.astype(jnp.float32)).astype(jnp.bfloat16)
    total = jnp.dot(low, had, preferred_element_type=jnp.float32)
    total = total + jnp.dot(middle, had, preferred_element_type=jnp.float32)
    total = total + jnp.dot(high, had, preferred_element_type=jnp.float32)
    return total * (1.0 / math.sqrt(BLOCK))


def kernel(
    a_ref, g_ref, w_ref, sign_ref, ig_ref, wg_ref,
    attn, grad, wq, others, staged, turned_ig, ig_v, acc, had_ref, eye, maxima, leaving, sib_in, summed, pieces, peaks, scale,
    scale_t, local_sem, a_s, a_r, g_s, g_r, w_s, w_r, h_s, h_r, o_s, o_r, i_s, i_r, m_s, m_r, q_s, q_r, p_s, p_r, c_s, c_r,
):
    dp, fsdp = lax.axis_index("dp"), lax.axis_index("fsdp")
    y, c = dp // 2, lax.rem(dp, 2)
    z, x = fsdp // SIDE, lax.rem(fsdp, SIDE)
    s = 1 - 2 * c
    off = [0, -s, s, 2]

    def mod(v):
        return lax.rem(v + 2 * SIDE, SIDE)

    def device(dx=0, dy=0, dz=0, dc=0):
        return (2 * mod(y + dy) + lax.rem(c + dc, 2), SIDE * mod(z + dz) + mod(x + dx))

    def remote(src, dst, send, recv, target):
        copy = pltpu.make_async_remote_copy(
            src_ref=src, dst_ref=dst, send_sem=send, recv_sem=recv, device_id=target, device_id_type=MESH
        )
        return copy

    sent = []

    def push(*args):
        copy = remote(*args)
        copy.start()
        sent.append(copy)
        return copy

    barrier = pltpu.get_barrier_semaphore()
    greeted = [device(dx=d) for d in range(1, SIDE)] + [device(dz=d) for d in range(1, SIDE)]
    greeted += [(lax.rem(dp + d, 8), fsdp) for d in range(1, 8)]
    for target in greeted:
        pl.semaphore_signal(barrier, inc=1, device_id=target, device_id_type=MESH)
    diagonal = x == y
    for k in range(SIDE):

        @pl.when(jnp.logical_not(jnp.logical_and(diagonal, k == y)))
        def _():
            pl.semaphore_signal(barrier, inc=1, device_id=(2 * k + c, SIDE * z + y), device_id_type=MESH)

    had_ref[...] = hadamard_signs()
    row = lax.broadcasted_iota(jnp.int32, (TOK, TOK), 0)
    col = lax.broadcasted_iota(jnp.int32, (TOK, TOK), 1)
    eye[...] = jnp.where(row == col, 1.0, 0.0).astype(eye.dtype)

    maxima[...] = jnp.zeros_like(maxima)
    pl.semaphore_wait(barrier, len(greeted) + SIDE - diagonal.astype(jnp.int32))

    depth = FEATURES // 2
    k_half = pl.ds(pl.multiple_of(depth * c, depth), depth)
    y_rows = pl.ds(pl.multiple_of(QUARTER * y, QUARTER), QUARTER)

    def w_chunk(pa, pb):
        on_z = lax.select(c == 1, mod(z + off[pa]), mod(z + off[pb]))
        on_x = lax.select(c == 1, mod(x + off[pb]), mod(x + off[pa]))
        return wq.at[pl.ds(pl.multiple_of(QUARTER * (SIDE * on_z + on_x), QUARTER), QUARTER), k_half]

    def along_a(d):
        return device(dx=lax.select(c == 1, 0, d), dz=lax.select(c == 1, d, 0))

    def along_b(d):
        return device(dx=lax.select(c == 1, d, 0), dz=lax.select(c == 1, 0, d))

    w_copies = {}

    def w_push(src, dst, landing, target):
        index = 4 * landing[1] + landing[0]
        w_copies[landing] = push(src, dst, w_s.at[index], w_r.at[index], target)

    w_own = w_ref.at[y_rows, k_half]
    w_push(w_own, w_chunk(0, 0), (1, 0), along_a(s))
    w_push(w_own, w_chunk(0, 0), (2, 0), along_a(-s))
    w_push(w_own, w_chunk(0, 0), (3, 0), along_a(2))
    w_push(w_own, w_chunk(0, 0), (0, 1), along_b(s))
    w_push(w_own, w_chunk(0, 0), (0, 2), along_b(-s))

    o_copies = [
        None,
        push(g_ref, others.at[1], o_s.at[0], o_r.at[0], device(dy=s)),
        push(g_ref, others.at[2], o_s.at[1], o_r.at[1], device(dy=-s)),
    ]

    def a_block(jx, kz):
        return attn.at[jx, pl.ds(TOK * kz, TOK)]

    def g_block(jx, kz):
        return grad.at[jx, pl.ds(TOK * kz, TOK)]

    def a_columns(owner):
        return a_ref.at[:, pl.ds(pl.multiple_of(TILE * owner, TILE), TILE)]

    def g_columns(owner):
        return g_ref.at[:, pl.ds(pl.multiple_of(TILE * owner, TILE), TILE)]

    a_copies, g_copies = {}, {}

    def a_push(src, landing, target):
        index = 4 * landing[0] + landing[1]
        a_copies[landing] = push(src, a_block(*landing), a_s.at[index], a_r.at[index], target)

    def g_push(src, landing, target):
        index = 4 * landing[0] + landing[1]
        g_copies[landing] = push(src, g_block(*landing), g_s.at[index], g_r.at[index], target)

    local = [
        pltpu.make_async_copy(a_columns(z), a_block(0, 0), local_sem.at[0]),
        pltpu.make_async_copy(g_columns(x), g_block(0, 0), local_sem.at[1]),
        pltpu.make_async_copy(g_ref, others.at[0], local_sem.at[2]),
        pltpu.make_async_copy(
            w_ref.at[y_rows, :],
            wq.at[pl.ds(pl.multiple_of(QUARTER * fsdp, QUARTER), QUARTER), :],
            local_sem.at[3],
        ),
    ]
    for copy in local:
        copy.start()
    for position, d in ((1, s), (2, -s), (3, 2)):
        a_push(a_columns(mod(z + d)), (0, position), device(dz=d))
        g_push(g_columns(mod(x + d)), (position, 0), device(dx=d))

    def a_spread(kz):
        a_push(a_block(0, kz), (1, kz), device(dx=s))
        a_push(a_block(0, kz), (2, kz), device(dx=-s))

    def g_spread(jx):
        g_push(g_block(jx, 0), (jx, 1), device(dz=s))
        g_push(g_block(jx, 0), (jx, 2), device(dz=-s))

    def own_blocks():
        local[0].wait()
        a_spread(0)
        local[1].wait()
        g_spread(0)

    def blocks(position):
        a_copies[0, position].wait_recv()
        a_spread(position)
        g_copies[position, 0].wait_recv()
        g_spread(position)

    shares = []

    def weight(pa, pb):
        w_copies[pa, pb].wait_recv()
        chunk = w_chunk(pa, pb)
        index = 4 * pb + pa
        if pb == 0:
            w_push(chunk, chunk, (pa, 1), along_b(s))
            w_push(chunk, chunk, (pa, 2), along_b(-s))
            if pa in ():
                w_push(chunk, chunk, (pa, 3), along_b(2))
        if pb == 1 and pa in (0, 1, 2, 3):
            w_push(chunk, chunk, (pa, 3), along_b(s))
        shares.append(push(chunk, chunk, h_s.at[index], h_r.at[index], device(dc=1)))

    def shared():
        local[2].wait()
        local[3].wait()
        for copy in shares:
            copy.wait_recv()

    def forward(i):
        a_copies[1, i].wait_recv()
        a_push(a_block(1, i), (3, i), device(dx=s))
        g_copies[i, 1].wait_recv()
        g_push(g_block(i, 1), (i, 3), device(dz=s))

    def pass_on():
        o_copies[1].wait_recv()
        o_copies.append(push(others.at[1], others.at[3], o_s.at[2], o_r.at[2], device(dy=s)))

    def partial_step(jx, low, high, first=False):
        def tile(m, carry):
            rows = pl.ds(pl.multiple_of(256 * m, 256), 256)
            value = lax.dot_general(
                attn[jx, TOK * low : TOK * high, rows],
                grad[jx, TOK * low : TOK * high, :],
                (((0,), (0,)), ((), ())),
                preferred_element_type=jnp.float32,
            )
            if first:
                acc[rows, :] = value
            else:
                acc[rows, :] += value
            return carry

        lax.fori_loop(0, TILE // 256, tile, 0)

    i_copies = []

    def slab(slot):
        if slot > 1:
            o_copies[slot].wait_recv()

        def tile(n, carry):
            rows = pl.ds(pl.multiple_of(HALF * n, HALF), HALF)
            shards = pl.ds(8 * n, 8)
            value = lax.dot_general(
                wq[rows, :], others[slot], (((1,), (1,)), ((), ())), preferred_element_type=jnp.float32
            )
            value = value.astype(staged.dtype).reshape(8, QUARTER, TOK)
            if slot == 0:
                turned_ig[shards, y_rows, :] = value
            else:
                staged[slot - 1, shards] = value
            return carry

        lax.fori_loop(0, TILE // HALF, tile, 0)
        if slot:
            landing = turned_ig.at[:, y_rows, :]
            i_copies.append(
                push(staged.at[slot - 1], landing, i_s.at[slot - 1], i_r.at[slot - 1], device(dy=off[slot]))
            )

    def write_input_grad():
        for copy in i_copies:
            copy.wait_recv()

        def tile(n, carry):
            value = lax.dot_general(
                eye[...],
                turned_ig[pl.ds(2 * n, 2)].reshape(HALF, TOK),
                (((1,), (1,)), ((), ())),
                preferred_element_type=jnp.float32,
            )
            ig_v[:, pl.ds(pl.multiple_of(HALF * n, HALF), HALF)] = value.astype(ig_v.dtype)
            return carry

        lax.fori_loop(0, FEATURES // HALF, tile, 0)
        ig_out.start()

    ig_out = pltpu.make_async_copy(ig_v, ig_ref, local_sem.at[4])

    weight(1, 0)
    weight(2, 0)
    weight(3, 0)
    weight(0, 1)
    weight(1, 1)
    weight(2, 1)
    weight(3, 1)
    own_blocks()
    weight(0, 2)
    weight(1, 2)
    weight(2, 2)
    weight(3, 2)
    pass_on()
    weight(0, 3)
    weight(1, 3)
    weight(2, 3)
    weight(3, 3)
    blocks(1)
    blocks(2)
    blocks(3)
    shared()
    slab(1)
    slab(2)
    slab(0)
    forward(0)
    forward(1)
    slab(3)
    forward(2)
    forward(3)
    partial_step(0, 0, 2, first=True)
    partial_step(1, 0, 2)

    for i in range(SIDE):
        a_copies[2, i].wait_recv()
        g_copies[i, 2].wait_recv()
    partial_step(0, 2, 3)
    partial_step(1, 2, 3)
    partial_step(2, 0, 3)
    for i in range(SIDE):
        a_copies[3, i].wait_recv()
        g_copies[i, 3].wait_recv()
        if i < 3:
            partial_step(i, 3, 4)
        partial_step(3, i, i + 1)


    def turn(pair, carry):
        columns = pl.ds(pl.multiple_of(2 * BLOCK * pair, 2 * BLOCK), 2 * BLOCK)
        signs = sign_ref[:, pl.ds(pl.multiple_of(TILE * x + 2 * BLOCK * pair, BLOCK), 2 * BLOCK)].astype(jnp.float32)
        for m in range(3):
            rows = slice(256 * m, 256 * m + 256)
            turned = rotate(acc[rows, columns] * signs, had_ref[...])
            acc[rows, columns] = turned
            size = jnp.abs(turned)
            lane = lax.broadcasted_iota(jnp.int32, (256, BLOCK), 1)
            first = jnp.max(size[:, :BLOCK], axis=1, keepdims=True)
            second = jnp.max(size[:, BLOCK:], axis=1, keepdims=True)
            found = jnp.where(lane == 2 * pair + 1, second, maxima[rows, :])
            maxima[rows, :] = jnp.where(lane == 2 * pair, first, found)
        return carry

    lax.fori_loop(0, 3, turn, 0)
    for r in range(TILE // BLOCK):
        span = slice(BLOCK * r, BLOCK * r + BLOCK)
        peaks[0, :, span] = jnp.transpose(maxima[span, :])[:8]
    met = [
        push(peaks.at[0], peaks.at[d], m_s.at[d], m_r.at[d], (lax.rem(dp + d, 8), fsdp)) for d in range(1, 8)
    ]
    for copy in met:
        copy.wait_recv()
    top = peaks[0]
    for d in range(1, 8):
        top = jnp.maximum(top, peaks[d])
    scale[0] = top + EPSILON

    for d in range(1, SIDE):

        @pl.when(diagonal)
        def _():
            remote(scale.at[0], scale.at[1], c_s.at[d], c_r.at[0], device(dx=d)).start()

    for r in range(TILE // BLOCK):
        span = slice(BLOCK * r, BLOCK * r + BLOCK)
        scale_t[span, :] = jnp.transpose(
            jnp.concatenate([127.0 / scale[0, :, span], jnp.ones((BLOCK - 8, BLOCK), jnp.float32)], axis=0)
        )

    def quarter(k):
        return mod(x + (2, 1, 3, 0)[k])

    def quarter_rows(k):
        return pl.ds(pl.multiple_of(SHARD * quarter(k), SHARD), SHARD)

    def quantize(target, side, k):
        rows = quarter_rows(k)
        for j in range(HALF // BLOCK):
            source = pl.ds(pl.multiple_of(HALF * side + BLOCK * j, BLOCK), BLOCK)
            factor = jnp.where(side == 0, scale_t[rows, j : j + 1], scale_t[rows, 3 + j : 4 + j])
            target[rows, BLOCK * j : BLOCK * j + BLOCK] = jnp.floor(acc[rows, source] * factor + 0.5).astype(target.dtype)

    def piece_copies(k):
        src = summed.at[quarter_rows(k), :]
        here = pltpu.make_async_copy(src, pieces.at[y], p_s.at[k])
        away = remote(src, pieces.at[y], p_s.at[k], p_r.at[y], (2 * x + c, SIDE * z + quarter(k)))
        return jnp.logical_and(diagonal, k == 3), here, away

    traded = []

    def finish(k):
        traded[k].wait_recv()
        rows = quarter_rows(k)
        summed[rows, :] += sib_in[rows, :]
        stays, here, away = piece_copies(k)
        pl.when(stays)(here.start)
        pl.when(jnp.logical_not(stays))(away.start)

    for k in range(SIDE):
        quantize(leaving, 1 - c, k)
        rows = quarter_rows(k)
        traded.append(push(leaving.at[rows, :], sib_in.at[rows, :], q_s.at[k], q_r.at[k], device(dc=1)))
        quantize(summed, c, k)
        if k:
            finish(k - 1)
    finish(SIDE - 1)

    write_input_grad()
    for copy in sent:
        copy.wait_send()

    @pl.when(jnp.logical_not(diagonal))
    def _():
        remote(scale.at[0], scale.at[1], c_s.at[0], c_r.at[0], device(dx=1)).wait_recv()

    @pl.when(diagonal)
    def _():
        scale[1] = scale[0]
        for d in range(1, SIDE):
            remote(scale.at[0], scale.at[1], c_s.at[d], c_r.at[0], device(dx=d)).wait_send()

    for r in range(TILE // BLOCK):
        span = slice(BLOCK * r, BLOCK * r + BLOCK)
        scale_t[span, :] = jnp.transpose(
            jnp.concatenate([scale[1, :, span] / 127.0, jnp.ones((BLOCK - 8, BLOCK), jnp.float32)], axis=0)
        )
    for k in range(SIDE):
        stays, here, away = piece_copies(k)
        pl.when(stays)(here.wait)
        pl.when(jnp.logical_not(stays))(away.wait_send)
    for k in range(SIDE):
        arrives = remote(pieces.at[k], pieces.at[k], p_s.at[k], p_r.at[k], device(dx=1))
        pl.when(jnp.logical_not(jnp.logical_and(diagonal, k == y)))(arrives.wait_recv)

    rows = pl.ds(pl.multiple_of(SHARD * x, SHARD), SHARD)
    factors = scale_t[rows, :]
    for j in range(HALF // BLOCK):
        columns = slice(BLOCK * j, BLOCK * j + BLOCK)
        total = pieces[0, :, columns].astype(jnp.float32)
        for k in range(1, SIDE):
            total = total + pieces[k, :, columns].astype(jnp.float32)
        factor = jnp.where(c == 0, factors[:, j : j + 1], factors[:, 3 + j : 4 + j])
        signs = sign_ref[:, pl.ds(pl.multiple_of(HALF * dp + BLOCK * j, BLOCK), BLOCK)].astype(jnp.float32)
        wg_ref[:, columns] = rotate(total * factor, had_ref[:BLOCK, :BLOCK]) * signs

    ig_out.wait()


def copy_kernel(ig_ref, wg_ref, ig_out, wg_out, ig_v, wg_v, sems):
    steps = [(wg_ref, wg_v, wg_out, 0)]
    for part in range(4):
        rows = pl.ds(part * TOK // 4, TOK // 4)
        steps.append((ig_ref.at[rows], ig_v.at[rows], ig_out.at[rows], 1 + part))
    for source, held, _, index in steps:
        pltpu.make_async_copy(source, held, sems.at[index]).start()
    for source, held, target, index in steps:
        pltpu.make_async_copy(source, held, sems.at[index]).wait()
        pltpu.make_async_copy(held, target, sems.at[8 + index]).start()
    for _, held, target, index in steps:
        pltpu.make_async_copy(held, target, sems.at[8 + index]).wait()


def body(attn_out, out_grad, weight, sign_vector):
    signs = sign_vector[None, :]
    hbm = pl.BlockSpec(memory_space=pl.ANY)
    vmem = pl.BlockSpec(memory_space=pltpu.VMEM)
    dma = pltpu.SemaphoreType.DMA
    made = pl.pallas_call(
        kernel,
        out_shape=(
            jax.ShapeDtypeStruct((TOK, FEATURES), jnp.bfloat16),
            jax.ShapeDtypeStruct((SHARD, HALF), jnp.float32),
        ),
        in_specs=[hbm, hbm, hbm, vmem],
        out_specs=(hbm, vmem),
        scratch_shapes=[
            pltpu.VMEM((SIDE, SIDE * TOK, TILE), jnp.bfloat16),
            pltpu.VMEM((SIDE, SIDE * TOK, TILE), jnp.bfloat16),
            pltpu.VMEM((TILE, FEATURES), jnp.bfloat16),
            pltpu.VMEM((SIDE, TOK, FEATURES), jnp.bfloat16),
            pltpu.VMEM((3, 16, QUARTER, TOK), jnp.bfloat16),
            pltpu.VMEM((16, SHARD, TOK), jnp.bfloat16),
            pltpu.VMEM((TOK, FEATURES), jnp.bfloat16),
            pltpu.VMEM((TILE, TILE), jnp.float32),
            pltpu.VMEM((2 * BLOCK, 2 * BLOCK), jnp.bfloat16),
            pltpu.VMEM((TOK, TOK), jnp.bfloat16),
            pltpu.VMEM((TILE, BLOCK), jnp.float32),
            pltpu.VMEM((TILE, HALF), jnp.bfloat16),
            pltpu.VMEM((TILE, HALF), jnp.bfloat16),
            pltpu.VMEM((TILE, HALF), jnp.bfloat16),
            pltpu.VMEM((SIDE, SHARD, HALF), jnp.bfloat16),
            pltpu.VMEM((8, 8, TILE), jnp.float32),
            pltpu.VMEM((2, 8, TILE), jnp.float32),
            pltpu.VMEM((TILE, BLOCK), jnp.float32),
            dma((5,)), dma((16,)), dma((16,)), dma((16,)), dma((16,)), dma((16,)), dma((16,)), dma((16,)), dma((16,)),
            dma((3,)), dma((3,)), dma((3,)), dma((3,)), dma((8,)), dma((8,)), dma((4,)), dma((4,)), dma((4,)), dma((4,)),
            dma((4,)), dma((1,)),
        ],
        compiler_params=pltpu.CompilerParams(
            collective_id=0, has_side_effects=True, vmem_limit_bytes=60 * 2**20
        ),
    )(attn_out, out_grad, weight, signs)
    return pl.pallas_call(
        copy_kernel,
        out_shape=tuple(jax.ShapeDtypeStruct(part.shape, part.dtype) for part in made),
        in_specs=[hbm, hbm],
        out_specs=(hbm, hbm),
        scratch_shapes=[
            pltpu.VMEM((TOK, FEATURES), jnp.bfloat16), pltpu.VMEM((SHARD, HALF), jnp.float32), dma((16,))
        ],
    )(*made)


def solution(mesh):
    in_specs = (P(("dp", "fsdp"), None), P(("dp", "fsdp"), None), P("fsdp", None), P())
    out_specs = (P(("dp", "fsdp"), None), P("fsdp", "dp"))
    return jax.shard_map(body, mesh=mesh, in_specs=in_specs, out_specs=out_specs, check_vma=False)
```

```python
import functools
import math

import jax
import jax.numpy as jnp
from jax import lax
from jax.experimental import pallas as pl
from jax.experimental.pallas import tpu as pltpu
from jax.sharding import PartitionSpec as P

BLOCK = 128
EPSILON = 1e-06
SIDE = 4
TOK = 256
SHARD = 192
TILE = 768
QUARTER = 48
HALF = 384
FEATURES = 3072
MESH = pl.DeviceIdType.MESH


def hadamard_signs():
    row = lax.broadcasted_iota(jnp.int32, (2 * BLOCK, 2 * BLOCK), 0)
    col = lax.broadcasted_iota(jnp.int32, (2 * BLOCK, 2 * BLOCK), 1)
    common = jnp.bitwise_and(row, col)
    parity = jnp.zeros((2 * BLOCK, 2 * BLOCK), jnp.int32)
    for shift in range(BLOCK.bit_length() - 1):
        parity = parity + jnp.bitwise_and(jnp.right_shift(common, shift), 1)
    signed = 1 - 2 * jnp.bitwise_and(parity, 1)
    signed = jnp.where(row // BLOCK == col // BLOCK, signed, 0)
    return signed.astype(jnp.float32).astype(jnp.bfloat16)


def rotate(value, had):
    high = value.astype(jnp.bfloat16)
    rest = value - high.astype(jnp.float32)
    middle = rest.astype(jnp.bfloat16)
    low = (rest - middle.astype(jnp.float32)).astype(jnp.bfloat16)
    total = jnp.dot(low, had, preferred_element_type=jnp.float32)
    total = total + jnp.dot(middle, had, preferred_element_type=jnp.float32)
    total = total + jnp.dot(high, had, preferred_element_type=jnp.float32)
    return total * (1.0 / math.sqrt(BLOCK))


def kernel(
    a_ref, g_ref, w_ref, sign_ref, ig_ref, wg_ref,
    attn, grad, wq, others, staged, turned_ig, ig_v, acc, had_ref, eye, maxima, leaving, sib_in, summed, pieces, peaks, scale,
    scale_t, local_sem, a_s, a_r, g_s, g_r, w_s, w_r, h_s, h_r, o_s, o_r, i_s, i_r, m_s, m_r, q_s, q_r, p_s, p_r, c_s, c_r,
):
    dp, fsdp = lax.axis_index("dp"), lax.axis_index("fsdp")
    y, c = dp // 2, lax.rem(dp, 2)
    z, x = fsdp // SIDE, lax.rem(fsdp, SIDE)
    s = 1 - 2 * c
    off = [0, -s, s, 2]

    def mod(v):
        return lax.rem(v + 2 * SIDE, SIDE)

    def device(dx=0, dy=0, dz=0, dc=0):
        return (2 * mod(y + dy) + lax.rem(c + dc, 2), SIDE * mod(z + dz) + mod(x + dx))

    def remote(src, dst, send, recv, target):
        copy = pltpu.make_async_remote_copy(
            src_ref=src, dst_ref=dst, send_sem=send, recv_sem=recv, device_id=target, device_id_type=MESH
        )
        return copy

    sent = []

    def push(*args):
        copy = remote(*args)
        copy.start()
        sent.append(copy)
        return copy

    barrier = pltpu.get_barrier_semaphore()
    greeted = [device(dx=d) for d in range(1, SIDE)] + [device(dz=d) for d in range(1, SIDE)]
    greeted += [(lax.rem(dp + d, 8), fsdp) for d in range(1, 8)]
    for target in greeted:
        pl.semaphore_signal(barrier, inc=1, device_id=target, device_id_type=MESH)
    diagonal = x == y
    for k in range(SIDE):

        @pl.when(jnp.logical_not(jnp.logical_and(diagonal, k == y)))
        def _():
            pl.semaphore_signal(barrier, inc=1, device_id=(2 * k + c, SIDE * z + y), device_id_type=MESH)

    had_ref[...] = hadamard_signs()
    row = lax.broadcasted_iota(jnp.int32, (TOK, TOK), 0)
    col = lax.broadcasted_iota(jnp.int32, (TOK, TOK), 1)
    eye[...] = jnp.where(row == col, 1.0, 0.0).astype(eye.dtype)

    maxima[...] = jnp.zeros_like(maxima)
    pl.semaphore_wait(barrier, len(greeted) + SIDE - diagonal.astype(jnp.int32))

    depth = FEATURES // 2
    k_half = pl.ds(pl.multiple_of(depth * c, depth), depth)
    y_rows = pl.ds(pl.multiple_of(QUARTER * y, QUARTER), QUARTER)

    def w_chunk(pa, pb):
        on_z = lax.select(c == 1, mod(z + off[pa]), mod(z + off[pb]))
        on_x = lax.select(c == 1, mod(x + off[pb]), mod(x + off[pa]))
        return wq.at[pl.ds(pl.multiple_of(QUARTER * (SIDE * on_z + on_x), QUARTER), QUARTER), k_half]

    def along_a(d):
        return device(dx=lax.select(c == 1, 0, d), dz=lax.select(c == 1, d, 0))

    def along_b(d):
        return device(dx=lax.select(c == 1, d, 0), dz=lax.select(c == 1, 0, d))

    w_copies = {}

    def w_push(src, dst, landing, target):
        index = 4 * landing[1] + landing[0]
        w_copies[landing] = push(src, dst, w_s.at[index], w_r.at[index], target)

    w_own = w_ref.at[y_rows, k_half]
    w_push(w_own, w_chunk(0, 0), (1, 0), along_a(s))
    w_push(w_own, w_chunk(0, 0), (2, 0), along_a(-s))
    w_push(w_own, w_chunk(0, 0), (3, 0), along_a(2))
    w_push(w_own, w_chunk(0, 0), (0, 1), along_b(s))
    w_push(w_own, w_chunk(0, 0), (0, 2), along_b(-s))

    o_copies = [
        None,
        push(g_ref, others.at[1], o_s.at[0], o_r.at[0], device(dy=s)),
        push(g_ref, others.at[2], o_s.at[1], o_r.at[1], device(dy=-s)),
    ]

    def a_block(jx, kz):
        return attn.at[jx, pl.ds(TOK * kz, TOK)]

    def g_block(jx, kz):
        return grad.at[jx, pl.ds(TOK * kz, TOK)]

    def a_columns(owner):
        return a_ref.at[:, pl.ds(pl.multiple_of(TILE * owner, TILE), TILE)]

    def g_columns(owner):
        return g_ref.at[:, pl.ds(pl.multiple_of(TILE * owner, TILE), TILE)]

    a_copies, g_copies = {}, {}

    def a_push(src, landing, target):
        index = 4 * landing[0] + landing[1]
        a_copies[landing] = push(src, a_block(*landing), a_s.at[index], a_r.at[index], target)

    def g_push(src, landing, target):
        index = 4 * landing[0] + landing[1]
        g_copies[landing] = push(src, g_block(*landing), g_s.at[index], g_r.at[index], target)

    local = [
        pltpu.make_async_copy(a_columns(z), a_block(0, 0), local_sem.at[0]),
        pltpu.make_async_copy(g_columns(x), g_block(0, 0), local_sem.at[1]),
        pltpu.make_async_copy(g_ref, others.at[0], local_sem.at[2]),
        pltpu.make_async_copy(
            w_ref.at[y_rows, :],
            wq.at[pl.ds(pl.multiple_of(QUARTER * fsdp, QUARTER), QUARTER), :],
            local_sem.at[3],
        ),
    ]
    for copy in local:
        copy.start()
    for position, d in ((1, s), (2, -s), (3, 2)):
        a_push(a_columns(mod(z + d)), (0, position), device(dz=d))
        g_push(g_columns(mod(x + d)), (position, 0), device(dx=d))

    def a_spread(kz):
        a_push(a_block(0, kz), (1, kz), device(dx=s))
        a_push(a_block(0, kz), (2, kz), device(dx=-s))

    def g_spread(jx):
        g_push(g_block(jx, 0), (jx, 1), device(dz=s))
        g_push(g_block(jx, 0), (jx, 2), device(dz=-s))

    def own_blocks():
        local[0].wait()
        a_spread(0)
        local[1].wait()
        g_spread(0)

    def blocks(position):
        a_copies[0, position].wait_recv()
        a_spread(position)
        g_copies[position, 0].wait_recv()
        g_spread(position)

    shares = []

    def weight(pa, pb):
        w_copies[pa, pb].wait_recv()
        chunk = w_chunk(pa, pb)
        index = 4 * pb + pa
        if pb == 0:
            w_push(chunk, chunk, (pa, 1), along_b(s))
            w_push(chunk, chunk, (pa, 2), along_b(-s))
            if pa in ():
                w_push(chunk, chunk, (pa, 3), along_b(2))
        if pb == 1 and pa in (0, 1, 2, 3):
            w_push(chunk, chunk, (pa, 3), along_b(s))
        shares.append(push(chunk, chunk, h_s.at[index], h_r.at[index], device(dc=1)))

    def shared():
        local[2].wait()
        local[3].wait()
        for copy in shares:
            copy.wait_recv()

    def forward(i):
        a_copies[1, i].wait_recv()
        a_push(a_block(1, i), (3, i), device(dx=s))
        g_copies[i, 1].wait_recv()
        g_push(g_block(i, 1), (i, 3), device(dz=s))

    def pass_on():
        o_copies[1].wait_recv()
        o_copies.append(push(others.at[1], others.at[3], o_s.at[2], o_r.at[2], device(dy=s)))

    def partial_step(jx, low, high, first=False):
        def tile(m, carry):
            rows = pl.ds(pl.multiple_of(256 * m, 256), 256)
            value = lax.dot_general(
                attn[jx, TOK * low : TOK * high, rows],
                grad[jx, TOK * low : TOK * high, :],
                (((0,), (0,)), ((), ())),
                preferred_element_type=jnp.float32,
            )
            if first:
                acc[rows, :] = value
            else:
                acc[rows, :] += value
            return carry

        lax.fori_loop(0, TILE // 256, tile, 0)

    i_copies = []

    def slab(slot):
        if slot > 1:
            o_copies[slot].wait_recv()

        def tile(n, carry):
            rows = pl.ds(pl.multiple_of(HALF * n, HALF), HALF)
            shards = pl.ds(8 * n, 8)
            value = lax.dot_general(
                wq[rows, :], others[slot], (((1,), (1,)), ((), ())), preferred_element_type=jnp.float32
            )
            value = value.astype(staged.dtype).reshape(8, QUARTER, TOK)
            if slot == 0:
                turned_ig[shards, y_rows, :] = value
            else:
                staged[slot - 1, shards] = value
            return carry

        lax.fori_loop(0, TILE // HALF, tile, 0)
        if slot:
            landing = turned_ig.at[:, y_rows, :]
            i_copies.append(
                push(staged.at[slot - 1], landing, i_s.at[slot - 1], i_r.at[slot - 1], device(dy=off[slot]))
            )

    def write_input_grad():
        for copy in i_copies:
            copy.wait_recv()

        def tile(n, carry):
            value = lax.dot_general(
                eye[...],
                turned_ig[pl.ds(2 * n, 2)].reshape(HALF, TOK),
                (((1,), (1,)), ((), ())),
                preferred_element_type=jnp.float32,
            )
            ig_v[:, pl.ds(pl.multiple_of(HALF * n, HALF), HALF)] = value.astype(ig_v.dtype)
            return carry

        lax.fori_loop(0, FEATURES // HALF, tile, 0)
        ig_out.start()

    ig_out = pltpu.make_async_copy(ig_v, ig_ref, local_sem.at[4])

    weight(1, 0)
    weight(2, 0)
    weight(3, 0)
    weight(0, 1)
    weight(1, 1)
    weight(2, 1)
    weight(3, 1)
    own_blocks()
    weight(0, 2)
    weight(1, 2)
    weight(2, 2)
    weight(3, 2)
    pass_on()
    weight(0, 3)
    weight(1, 3)
    weight(2, 3)
    weight(3, 3)
    blocks(1)
    blocks(2)
    blocks(3)
    shared()
    slab(1)
    slab(2)
    slab(0)
    forward(0)
    forward(1)
    slab(3)
    forward(2)
    forward(3)
    partial_step(0, 0, 2, first=True)
    partial_step(1, 0, 2)

    for i in range(SIDE):
        a_copies[2, i].wait_recv()
        g_copies[i, 2].wait_recv()
    partial_step(0, 2, 3)
    partial_step(1, 2, 3)
    partial_step(2, 0, 3)
    for i in range(SIDE):
        a_copies[3, i].wait_recv()
        g_copies[i, 3].wait_recv()
        if i < 3:
            partial_step(i, 3, 4)
        partial_step(3, i, i + 1)


    def turn(pair, carry):
        columns = pl.ds(pl.multiple_of(2 * BLOCK * pair, 2 * BLOCK), 2 * BLOCK)
        signs = sign_ref[:, pl.ds(pl.multiple_of(TILE * x + 2 * BLOCK * pair, BLOCK), 2 * BLOCK)].astype(jnp.float32)
        for m in range(3):
            rows = slice(256 * m, 256 * m + 256)
            turned = rotate(acc[rows, columns] * signs, had_ref[...])
            acc[rows, columns] = turned
            size = jnp.abs(turned)
            lane = lax.broadcasted_iota(jnp.int32, (256, BLOCK), 1)
            first = jnp.max(size[:, :BLOCK], axis=1, keepdims=True)
            second = jnp.max(size[:, BLOCK:], axis=1, keepdims=True)
            found = jnp.where(lane == 2 * pair + 1, second, maxima[rows, :])
            maxima[rows, :] = jnp.where(lane == 2 * pair, first, found)
        return carry

    for pair in range(3):
        turn(pair, 0)
    for r in range(TILE // BLOCK):
        span = slice(BLOCK * r, BLOCK * r + BLOCK)
        peaks[0, :, span] = jnp.transpose(maxima[span, :])[:8]
    met = [
        push(peaks.at[0], peaks.at[d], m_s.at[d], m_r.at[d], (lax.rem(dp + d, 8), fsdp)) for d in range(1, 8)
    ]
    for copy in met:
        copy.wait_recv()
    top = peaks[0]
    for d in range(1, 8):
        top = jnp.maximum(top, peaks[d])
    scale[0] = top + EPSILON

    for d in range(1, SIDE):

        @pl.when(diagonal)
        def _():
            remote(scale.at[0], scale.at[1], c_s.at[d], c_r.at[0], device(dx=d)).start()

    for r in range(TILE // BLOCK):
        span = slice(BLOCK * r, BLOCK * r + BLOCK)
        scale_t[span, :] = jnp.transpose(
            jnp.concatenate([127.0 / scale[0, :, span], jnp.ones((BLOCK - 8, BLOCK), jnp.float32)], axis=0)
        )

    def quarter(k):
        return mod(x + (2, 1, 3, 0)[k])

    def quarter_rows(k):
        return pl.ds(pl.multiple_of(SHARD * quarter(k), SHARD), SHARD)

    def quantize(target, side, k):
        rows = quarter_rows(k)
        for j in range(HALF // BLOCK):
            source = pl.ds(pl.multiple_of(HALF * side + BLOCK * j, BLOCK), BLOCK)
            factor = jnp.where(side == 0, scale_t[rows, j : j + 1], scale_t[rows, 3 + j : 4 + j])
            target[rows, BLOCK * j : BLOCK * j + BLOCK] = jnp.floor(acc[rows, source] * factor + 0.5).astype(target.dtype)

    def piece_copies(k):
        src = summed.at[quarter_rows(k), :]
        here = pltpu.make_async_copy(src, pieces.at[y], p_s.at[k])
        away = remote(src, pieces.at[y], p_s.at[k], p_r.at[y], (2 * x + c, SIDE * z + quarter(k)))
        return jnp.logical_and(diagonal, k == 3), here, away

    traded = []

    def finish(k):
        traded[k].wait_recv()
        rows = quarter_rows(k)
        summed[rows, :] += sib_in[rows, :]
        stays, here, away = piece_copies(k)
        pl.when(stays)(here.start)
        pl.when(jnp.logical_not(stays))(away.start)

    for k in range(SIDE):
        quantize(leaving, 1 - c, k)
        rows = quarter_rows(k)
        traded.append(push(leaving.at[rows, :], sib_in.at[rows, :], q_s.at[k], q_r.at[k], device(dc=1)))
        quantize(summed, c, k)
        if k:
            finish(k - 1)
    finish(SIDE - 1)

    write_input_grad()
    for copy in sent:
        copy.wait_send()

    @pl.when(jnp.logical_not(diagonal))
    def _():
        remote(scale.at[0], scale.at[1], c_s.at[0], c_r.at[0], device(dx=1)).wait_recv()

    @pl.when(diagonal)
    def _():
        scale[1] = scale[0]
        for d in range(1, SIDE):
            remote(scale.at[0], scale.at[1], c_s.at[d], c_r.at[0], device(dx=d)).wait_send()

    for r in range(TILE // BLOCK):
        span = slice(BLOCK * r, BLOCK * r + BLOCK)
        scale_t[span, :] = jnp.transpose(
            jnp.concatenate([scale[1, :, span] / 127.0, jnp.ones((BLOCK - 8, BLOCK), jnp.float32)], axis=0)
        )
    for k in range(SIDE):
        stays, here, away = piece_copies(k)
        pl.when(stays)(here.wait)
        pl.when(jnp.logical_not(stays))(away.wait_send)
    for k in range(SIDE):
        arrives = remote(pieces.at[k], pieces.at[k], p_s.at[k], p_r.at[k], device(dx=1))
        pl.when(jnp.logical_not(jnp.logical_and(diagonal, k == y)))(arrives.wait_recv)

    rows = pl.ds(pl.multiple_of(SHARD * x, SHARD), SHARD)
    factors = scale_t[rows, :]
    for j in range(HALF // BLOCK):
        columns = slice(BLOCK * j, BLOCK * j + BLOCK)
        total = pieces[0, :, columns].astype(jnp.float32)
        for k in range(1, SIDE):
            total = total + pieces[k, :, columns].astype(jnp.float32)
        factor = jnp.where(c == 0, factors[:, j : j + 1], factors[:, 3 + j : 4 + j])
        signs = sign_ref[:, pl.ds(pl.multiple_of(HALF * dp + BLOCK * j, BLOCK), BLOCK)].astype(jnp.float32)
        wg_ref[:, columns] = rotate(total * factor, had_ref[:BLOCK, :BLOCK]) * signs

    ig_out.wait()


def copy_kernel(ig_ref, wg_ref, ig_out, wg_out, ig_v, wg_v, sems):
    steps = [(wg_ref, wg_v, wg_out, 0)]
    for part in range(4):
        rows = pl.ds(part * TOK // 4, TOK // 4)
        steps.append((ig_ref.at[rows], ig_v.at[rows], ig_out.at[rows], 1 + part))
    for source, held, _, index in steps:
        pltpu.make_async_copy(source, held, sems.at[index]).start()
    for source, held, target, index in steps:
        pltpu.make_async_copy(source, held, sems.at[index]).wait()
        pltpu.make_async_copy(held, target, sems.at[8 + index]).start()
    for _, held, target, index in steps:
        pltpu.make_async_copy(held, target, sems.at[8 + index]).wait()


def body(attn_out, out_grad, weight, sign_vector):
    signs = sign_vector[None, :]
    hbm = pl.BlockSpec(memory_space=pl.ANY)
    vmem = pl.BlockSpec(memory_space=pltpu.VMEM)
    dma = pltpu.SemaphoreType.DMA
    made = pl.pallas_call(
        kernel,
        out_shape=(
            jax.ShapeDtypeStruct((TOK, FEATURES), jnp.bfloat16),
            jax.ShapeDtypeStruct((SHARD, HALF), jnp.float32),
        ),
        in_specs=[hbm, hbm, hbm, vmem],
        out_specs=(hbm, vmem),
        scratch_shapes=[
            pltpu.VMEM((SIDE, SIDE * TOK, TILE), jnp.bfloat16),
            pltpu.VMEM((SIDE, SIDE * TOK, TILE), jnp.bfloat16),
            pltpu.VMEM((TILE, FEATURES), jnp.bfloat16),
            pltpu.VMEM((SIDE, TOK, FEATURES), jnp.bfloat16),
            pltpu.VMEM((3, 16, QUARTER, TOK), jnp.bfloat16),
            pltpu.VMEM((16, SHARD, TOK), jnp.bfloat16),
            pltpu.VMEM((TOK, FEATURES), jnp.bfloat16),
            pltpu.VMEM((TILE, TILE), jnp.float32),
            pltpu.VMEM((2 * BLOCK, 2 * BLOCK), jnp.bfloat16),
            pltpu.VMEM((TOK, TOK), jnp.bfloat16),
            pltpu.VMEM((TILE, BLOCK), jnp.float32),
            pltpu.VMEM((TILE, HALF), jnp.bfloat16),
            pltpu.VMEM((TILE, HALF), jnp.bfloat16),
            pltpu.VMEM((TILE, HALF), jnp.bfloat16),
            pltpu.VMEM((SIDE, SHARD, HALF), jnp.bfloat16),
            pltpu.VMEM((8, 8, TILE), jnp.float32),
            pltpu.VMEM((2, 8, TILE), jnp.float32),
            pltpu.VMEM((TILE, BLOCK), jnp.float32),
            dma((5,)), dma((16,)), dma((16,)), dma((16,)), dma((16,)), dma((16,)), dma((16,)), dma((16,)), dma((16,)),
            dma((3,)), dma((3,)), dma((3,)), dma((3,)), dma((8,)), dma((8,)), dma((4,)), dma((4,)), dma((4,)), dma((4,)),
            dma((4,)), dma((1,)),
        ],
        compiler_params=pltpu.CompilerParams(
            collective_id=0, has_side_effects=True, vmem_limit_bytes=60 * 2**20
        ),
    )(attn_out, out_grad, weight, signs)
    return pl.pallas_call(
        copy_kernel,
        out_shape=tuple(jax.ShapeDtypeStruct(part.shape, part.dtype) for part in made),
        in_specs=[hbm, hbm],
        out_specs=(hbm, hbm),
        scratch_shapes=[
            pltpu.VMEM((TOK, FEATURES), jnp.bfloat16), pltpu.VMEM((SHARD, HALF), jnp.float32), dma((16,))
        ],
    )(*made)


def solution(mesh):
    in_specs = (P(("dp", "fsdp"), None), P(("dp", "fsdp"), None), P("fsdp", None), P())
    out_specs = (P(("dp", "fsdp"), None), P("fsdp", "dp"))
    return jax.shard_map(body, mesh=mesh, in_specs=in_specs, out_specs=out_specs, check_vma=False)
```

```python
import functools
import math

import jax
import jax.numpy as jnp
from jax import lax
from jax.experimental import pallas as pl
from jax.experimental.pallas import tpu as pltpu
from jax.sharding import PartitionSpec as P

BLOCK = 128
EPSILON = 1e-06
SIDE = 4
TOK = 256
SHARD = 192
TILE = 768
QUARTER = 48
HALF = 384
FEATURES = 3072
MESH = pl.DeviceIdType.MESH


def hadamard_signs():
    row = lax.broadcasted_iota(jnp.int32, (2 * BLOCK, 2 * BLOCK), 0)
    col = lax.broadcasted_iota(jnp.int32, (2 * BLOCK, 2 * BLOCK), 1)
    common = jnp.bitwise_and(row, col)
    parity = jnp.zeros((2 * BLOCK, 2 * BLOCK), jnp.int32)
    for shift in range(BLOCK.bit_length() - 1):
        parity = parity + jnp.bitwise_and(jnp.right_shift(common, shift), 1)
    signed = 1 - 2 * jnp.bitwise_and(parity, 1)
    signed = jnp.where(row // BLOCK == col // BLOCK, signed, 0)
    return signed.astype(jnp.float32).astype(jnp.bfloat16)


def rotate(value, had):
    high = value.astype(jnp.bfloat16)
    rest = value - high.astype(jnp.float32)
    middle = rest.astype(jnp.bfloat16)
    low = (rest - middle.astype(jnp.float32)).astype(jnp.bfloat16)
    total = jnp.dot(low, had, preferred_element_type=jnp.float32)
    total = total + jnp.dot(middle, had, preferred_element_type=jnp.float32)
    total = total + jnp.dot(high, had, preferred_element_type=jnp.float32)
    return total * (1.0 / math.sqrt(BLOCK))


def kernel(
    a_ref, g_ref, w_ref, sign_ref, ig_ref, wg_ref,
    attn, grad, wq, others, staged, turned_ig, ig_v, acc, had_ref, eye, maxima, leaving, sib_in, summed, pieces, peaks, scale,
    scale_t, local_sem, a_s, a_r, g_s, g_r, w_s, w_r, h_s, h_r, o_s, o_r, i_s, i_r, m_s, m_r, q_s, q_r, p_s, p_r, c_s, c_r,
):
    dp, fsdp = lax.axis_index("dp"), lax.axis_index("fsdp")
    y, c = dp // 2, lax.rem(dp, 2)
    z, x = fsdp // SIDE, lax.rem(fsdp, SIDE)
    s = 1 - 2 * c
    off = [0, -s, s, 2]

    def mod(v):
        return lax.rem(v + 2 * SIDE, SIDE)

    def device(dx=0, dy=0, dz=0, dc=0):
        return (2 * mod(y + dy) + lax.rem(c + dc, 2), SIDE * mod(z + dz) + mod(x + dx))

    def remote(src, dst, send, recv, target):
        copy = pltpu.make_async_remote_copy(
            src_ref=src, dst_ref=dst, send_sem=send, recv_sem=recv, device_id=target, device_id_type=MESH
        )
        return copy

    sent = []

    def push(*args):
        copy = remote(*args)
        copy.start()
        sent.append(copy)
        return copy

    barrier = pltpu.get_barrier_semaphore()
    greeted = [device(dx=d) for d in range(1, SIDE)] + [device(dz=d) for d in range(1, SIDE)]
    greeted += [(lax.rem(dp + d, 8), fsdp) for d in range(1, 8)]
    for target in greeted:
        pl.semaphore_signal(barrier, inc=1, device_id=target, device_id_type=MESH)
    diagonal = x == y
    for k in range(SIDE):

        @pl.when(jnp.logical_not(jnp.logical_and(diagonal, k == y)))
        def _():
            pl.semaphore_signal(barrier, inc=1, device_id=(2 * k + c, SIDE * z + y), device_id_type=MESH)

    had_ref[...] = hadamard_signs()
    row = lax.broadcasted_iota(jnp.int32, (TOK, TOK), 0)
    col = lax.broadcasted_iota(jnp.int32, (TOK, TOK), 1)
    eye[...] = jnp.where(row == col, 1.0, 0.0).astype(eye.dtype)

    maxima[...] = jnp.zeros_like(maxima)
    pl.semaphore_wait(barrier, len(greeted) + SIDE - diagonal.astype(jnp.int32))

    depth = FEATURES // 2
    k_half = pl.ds(pl.multiple_of(depth * c, depth), depth)
    y_rows = pl.ds(pl.multiple_of(QUARTER * y, QUARTER), QUARTER)

    def w_chunk(pa, pb):
        on_z = lax.select(c == 1, mod(z + off[pa]), mod(z + off[pb]))
        on_x = lax.select(c == 1, mod(x + off[pb]), mod(x + off[pa]))
        return wq.at[pl.ds(pl.multiple_of(QUARTER * (SIDE * on_z + on_x), QUARTER), QUARTER), k_half]

    def along_a(d):
        return device(dx=lax.select(c == 1, 0, d), dz=lax.select(c == 1, d, 0))

    def along_b(d):
        return device(dx=lax.select(c == 1, d, 0), dz=lax.select(c == 1, 0, d))

    w_copies = {}

    def w_push(src, dst, landing, target):
        index = 4 * landing[1] + landing[0]
        w_copies[landing] = push(src, dst, w_s.at[index], w_r.at[index], target)

    w_own = w_ref.at[y_rows, k_half]
    w_push(w_own, w_chunk(0, 0), (1, 0), along_a(s))
    w_push(w_own, w_chunk(0, 0), (2, 0), along_a(-s))
    w_push(w_own, w_chunk(0, 0), (3, 0), along_a(2))
    w_push(w_own, w_chunk(0, 0), (0, 1), along_b(s))
    w_push(w_own, w_chunk(0, 0), (0, 2), along_b(-s))

    o_copies = [
        None,
        push(g_ref, others.at[1], o_s.at[0], o_r.at[0], device(dy=s)),
        push(g_ref, others.at[2], o_s.at[1], o_r.at[1], device(dy=-s)),
    ]

    def a_block(jx, kz):
        return attn.at[jx, pl.ds(TOK * kz, TOK)]

    def g_block(jx, kz):
        return grad.at[jx, pl.ds(TOK * kz, TOK)]

    def a_columns(owner):
        return a_ref.at[:, pl.ds(pl.multiple_of(TILE * owner, TILE), TILE)]

    def g_columns(owner):
        return g_ref.at[:, pl.ds(pl.multiple_of(TILE * owner, TILE), TILE)]

    a_copies, g_copies = {}, {}

    def a_push(src, landing, target):
        index = 4 * landing[0] + landing[1]
        a_copies[landing] = push(src, a_block(*landing), a_s.at[index], a_r.at[index], target)

    def g_push(src, landing, target):
        index = 4 * landing[0] + landing[1]
        g_copies[landing] = push(src, g_block(*landing), g_s.at[index], g_r.at[index], target)

    local = [
        pltpu.make_async_copy(a_columns(z), a_block(0, 0), local_sem.at[0]),
        pltpu.make_async_copy(g_columns(x), g_block(0, 0), local_sem.at[1]),
        pltpu.make_async_copy(g_ref, others.at[0], local_sem.at[2]),
        pltpu.make_async_copy(
            w_ref.at[y_rows, :],
            wq.at[pl.ds(pl.multiple_of(QUARTER * fsdp, QUARTER), QUARTER), :],
            local_sem.at[3],
        ),
    ]
    for copy in local:
        copy.start()
    for position, d in ((1, s), (2, -s), (3, 2)):
        a_push(a_columns(mod(z + d)), (0, position), device(dz=d))
        g_push(g_columns(mod(x + d)), (position, 0), device(dx=d))

    def a_spread(kz):
        a_push(a_block(0, kz), (1, kz), device(dx=s))
        a_push(a_block(0, kz), (2, kz), device(dx=-s))

    def g_spread(jx):
        g_push(g_block(jx, 0), (jx, 1), device(dz=s))
        g_push(g_block(jx, 0), (jx, 2), device(dz=-s))

    def own_blocks():
        local[0].wait()
        a_spread(0)
        local[1].wait()
        g_spread(0)

    def blocks(position):
        a_copies[0, position].wait_recv()
        a_spread(position)
        g_copies[position, 0].wait_recv()
        g_spread(position)

    shares = []

    def weight(pa, pb):
        w_copies[pa, pb].wait_recv()
        chunk = w_chunk(pa, pb)
        index = 4 * pb + pa
        if pb == 0:
            w_push(chunk, chunk, (pa, 1), along_b(s))
            w_push(chunk, chunk, (pa, 2), along_b(-s))
            if pa in ():
                w_push(chunk, chunk, (pa, 3), along_b(2))
        if pb == 1 and pa in (0, 1, 2, 3):
            w_push(chunk, chunk, (pa, 3), along_b(s))
        shares.append(push(chunk, chunk, h_s.at[index], h_r.at[index], device(dc=1)))

    def shared():
        local[2].wait()
        local[3].wait()
        for copy in shares:
            copy.wait_recv()

    def forward(i):
        a_copies[1, i].wait_recv()
        a_push(a_block(1, i), (3, i), device(dx=s))
        g_copies[i, 1].wait_recv()
        g_push(g_block(i, 1), (i, 3), device(dz=s))

    def pass_on():
        o_copies[1].wait_recv()
        o_copies.append(push(others.at[1], others.at[3], o_s.at[2], o_r.at[2], device(dy=s)))

    def partial_step(jx, low, high, first=False):
        def tile(m, carry):
            rows = pl.ds(256 * m if isinstance(m, int) else pl.multiple_of(256 * m, 256), 256)
            value = lax.dot_general(
                attn[jx, TOK * low : TOK * high, rows],
                grad[jx, TOK * low : TOK * high, :],
                (((0,), (0,)), ((), ())),
                preferred_element_type=jnp.float32,
            )
            if first:
                acc[rows, :] = value
            else:
                acc[rows, :] += value
            return carry

        if (jx, low) == (3, 3):
            for m in range(TILE // 256):
                tile(m, 0)
        else:
            lax.fori_loop(0, TILE // 256, tile, 0)

    i_copies = []

    def slab(slot):
        if slot > 1:
            o_copies[slot].wait_recv()

        def tile(n, carry):
            rows = pl.ds(pl.multiple_of(HALF * n, HALF), HALF)
            shards = pl.ds(8 * n, 8)
            value = lax.dot_general(
                wq[rows, :], others[slot], (((1,), (1,)), ((), ())), preferred_element_type=jnp.float32
            )
            value = value.astype(staged.dtype).reshape(8, QUARTER, TOK)
            if slot == 0:
                turned_ig[shards, y_rows, :] = value
            else:
                staged[slot - 1, shards] = value
            return carry

        lax.fori_loop(0, TILE // HALF, tile, 0)
        if slot:
            landing = turned_ig.at[:, y_rows, :]
            i_copies.append(
                push(staged.at[slot - 1], landing, i_s.at[slot - 1], i_r.at[slot - 1], device(dy=off[slot]))
            )

    def write_input_grad():
        for copy in i_copies:
            copy.wait_recv()

        def tile(n, carry):
            value = lax.dot_general(
                eye[...],
                turned_ig[pl.ds(2 * n, 2)].reshape(HALF, TOK),
                (((1,), (1,)), ((), ())),
                preferred_element_type=jnp.float32,
            )
            ig_v[:, pl.ds(pl.multiple_of(HALF * n, HALF), HALF)] = value.astype(ig_v.dtype)
            return carry

        lax.fori_loop(0, FEATURES // HALF, tile, 0)
        ig_out.start()

    ig_out = pltpu.make_async_copy(ig_v, ig_ref, local_sem.at[4])

    weight(1, 0)
    weight(2, 0)
    weight(3, 0)
    weight(0, 1)
    weight(1, 1)
    weight(2, 1)
    weight(3, 1)
    own_blocks()
    weight(0, 2)
    weight(1, 2)
    weight(2, 2)
    weight(3, 2)
    pass_on()
    weight(0, 3)
    weight(1, 3)
    weight(2, 3)
    weight(3, 3)
    blocks(1)
    blocks(2)
    blocks(3)
    shared()
    slab(1)
    slab(2)
    slab(0)
    forward(0)
    forward(1)
    slab(3)
    forward(2)
    forward(3)
    partial_step(0, 0, 2, first=True)
    partial_step(1, 0, 2)

    for i in range(SIDE):
        a_copies[2, i].wait_recv()
        g_copies[i, 2].wait_recv()
    partial_step(0, 2, 3)
    partial_step(1, 2, 3)
    partial_step(2, 0, 3)
    for i in range(SIDE):
        a_copies[3, i].wait_recv()
        g_copies[i, 3].wait_recv()
        if i < 3:
            partial_step(i, 3, 4)
        partial_step(3, i, i + 1)


    def turn(pair, carry):
        columns = pl.ds(pl.multiple_of(2 * BLOCK * pair, 2 * BLOCK), 2 * BLOCK)
        signs = sign_ref[:, pl.ds(pl.multiple_of(TILE * x + 2 * BLOCK * pair, BLOCK), 2 * BLOCK)].astype(jnp.float32)
        for m in range(3):
            rows = slice(256 * m, 256 * m + 256)
            turned = rotate(acc[rows, columns] * signs, had_ref[...])
            acc[rows, columns] = turned
            size = jnp.abs(turned)
            lane = lax.broadcasted_iota(jnp.int32, (256, BLOCK), 1)
            first = jnp.max(size[:, :BLOCK], axis=1, keepdims=True)
            second = jnp.max(size[:, BLOCK:], axis=1, keepdims=True)
            found = jnp.where(lane == 2 * pair + 1, second, maxima[rows, :])
            maxima[rows, :] = jnp.where(lane == 2 * pair, first, found)
        return carry

    for pair in range(3):
        turn(pair, 0)
    for r in range(TILE // BLOCK):
        span = slice(BLOCK * r, BLOCK * r + BLOCK)
        peaks[0, :, span] = jnp.transpose(maxima[span, :])[:8]
    met = [
        push(peaks.at[0], peaks.at[d], m_s.at[d], m_r.at[d], (lax.rem(dp + d, 8), fsdp)) for d in range(1, 8)
    ]
    for copy in met:
        copy.wait_recv()
    top = peaks[0]
    for d in range(1, 8):
        top = jnp.maximum(top, peaks[d])
    scale[0] = top + EPSILON

    for d in range(1, SIDE):

        @pl.when(diagonal)
        def _():
            remote(scale.at[0], scale.at[1], c_s.at[d], c_r.at[0], device(dx=d)).start()

    for r in range(TILE // BLOCK):
        span = slice(BLOCK * r, BLOCK * r + BLOCK)
        scale_t[span, :] = jnp.transpose(
            jnp.concatenate([127.0 / scale[0, :, span], jnp.ones((BLOCK - 8, BLOCK), jnp.float32)], axis=0)
        )

    def quarter(k):
        return mod(x + (2, 1, 3, 0)[k])

    def quarter_rows(k):
        return pl.ds(pl.multiple_of(SHARD * quarter(k), SHARD), SHARD)

    def quantize(target, side, k):
        rows = quarter_rows(k)
        for j in range(HALF // BLOCK):
            source = pl.ds(pl.multiple_of(HALF * side + BLOCK * j, BLOCK), BLOCK)
            factor = jnp.where(side == 0, scale_t[rows, j : j + 1], scale_t[rows, 3 + j : 4 + j])
            target[rows, BLOCK * j : BLOCK * j + BLOCK] = jnp.floor(acc[rows, source] * factor + 0.5).astype(target.dtype)

    def piece_copies(k):
        src = summed.at[quarter_rows(k), :]
        here = pltpu.make_async_copy(src, pieces.at[y], p_s.at[k])
        away = remote(src, pieces.at[y], p_s.at[k], p_r.at[y], (2 * x + c, SIDE * z + quarter(k)))
        return jnp.logical_and(diagonal, k == 3), here, away

    traded = []

    def finish(k):
        traded[k].wait_recv()
        rows = quarter_rows(k)
        summed[rows, :] += sib_in[rows, :]
        stays, here, away = piece_copies(k)
        pl.when(stays)(here.start)
        pl.when(jnp.logical_not(stays))(away.start)

    for k in range(SIDE):
        quantize(leaving, 1 - c, k)
        rows = quarter_rows(k)
        traded.append(push(leaving.at[rows, :], sib_in.at[rows, :], q_s.at[k], q_r.at[k], device(dc=1)))
        quantize(summed, c, k)
        if k:
            finish(k - 1)
    finish(SIDE - 1)

    write_input_grad()
    for copy in sent:
        copy.wait_send()

    @pl.when(jnp.logical_not(diagonal))
    def _():
        remote(scale.at[0], scale.at[1], c_s.at[0], c_r.at[0], device(dx=1)).wait_recv()

    @pl.when(diagonal)
    def _():
        scale[1] = scale[0]
        for d in range(1, SIDE):
            remote(scale.at[0], scale.at[1], c_s.at[d], c_r.at[0], device(dx=d)).wait_send()

    for r in range(TILE // BLOCK):
        span = slice(BLOCK * r, BLOCK * r + BLOCK)
        scale_t[span, :] = jnp.transpose(
            jnp.concatenate([scale[1, :, span] / 127.0, jnp.ones((BLOCK - 8, BLOCK), jnp.float32)], axis=0)
        )
    for k in range(SIDE):
        stays, here, away = piece_copies(k)
        pl.when(stays)(here.wait)
        pl.when(jnp.logical_not(stays))(away.wait_send)
    for k in range(SIDE):
        arrives = remote(pieces.at[k], pieces.at[k], p_s.at[k], p_r.at[k], device(dx=1))
        pl.when(jnp.logical_not(jnp.logical_and(diagonal, k == y)))(arrives.wait_recv)

    rows = pl.ds(pl.multiple_of(SHARD * x, SHARD), SHARD)
    factors = scale_t[rows, :]
    for j in range(HALF // BLOCK):
        columns = slice(BLOCK * j, BLOCK * j + BLOCK)
        total = pieces[0, :, columns].astype(jnp.float32)
        for k in range(1, SIDE):
            total = total + pieces[k, :, columns].astype(jnp.float32)
        factor = jnp.where(c == 0, factors[:, j : j + 1], factors[:, 3 + j : 4 + j])
        signs = sign_ref[:, pl.ds(pl.multiple_of(HALF * dp + BLOCK * j, BLOCK), BLOCK)].astype(jnp.float32)
        wg_ref[:, columns] = rotate(total * factor, had_ref[:BLOCK, :BLOCK]) * signs

    ig_out.wait()


def copy_kernel(ig_ref, wg_ref, ig_out, wg_out, ig_v, wg_v, sems):
    steps = [(wg_ref, wg_v, wg_out, 0)]
    for part in range(4):
        rows = pl.ds(part * TOK // 4, TOK // 4)
        steps.append((ig_ref.at[rows], ig_v.at[rows], ig_out.at[rows], 1 + part))
    for source, held, _, index in steps:
        pltpu.make_async_copy(source, held, sems.at[index]).start()
    for source, held, target, index in steps:
        pltpu.make_async_copy(source, held, sems.at[index]).wait()
        pltpu.make_async_copy(held, target, sems.at[8 + index]).start()
    for _, held, target, index in steps:
        pltpu.make_async_copy(held, target, sems.at[8 + index]).wait()


def body(attn_out, out_grad, weight, sign_vector):
    signs = sign_vector[None, :]
    hbm = pl.BlockSpec(memory_space=pl.ANY)
    vmem = pl.BlockSpec(memory_space=pltpu.VMEM)
    dma = pltpu.SemaphoreType.DMA
    made = pl.pallas_call(
        kernel,
        out_shape=(
            jax.ShapeDtypeStruct((TOK, FEATURES), jnp.bfloat16),
            jax.ShapeDtypeStruct((SHARD, HALF), jnp.float32),
        ),
        in_specs=[hbm, hbm, hbm, vmem],
        out_specs=(hbm, vmem),
        scratch_shapes=[
            pltpu.VMEM((SIDE, SIDE * TOK, TILE), jnp.bfloat16),
            pltpu.VMEM((SIDE, SIDE * TOK, TILE), jnp.bfloat16),
            pltpu.VMEM((TILE, FEATURES), jnp.bfloat16),
            pltpu.VMEM((SIDE, TOK, FEATURES), jnp.bfloat16),
            pltpu.VMEM((3, 16, QUARTER, TOK), jnp.bfloat16),
            pltpu.VMEM((16, SHARD, TOK), jnp.bfloat16),
            pltpu.VMEM((TOK, FEATURES), jnp.bfloat16),
            pltpu.VMEM((TILE, TILE), jnp.float32),
            pltpu.VMEM((2 * BLOCK, 2 * BLOCK), jnp.bfloat16),
            pltpu.VMEM((TOK, TOK), jnp.bfloat16),
            pltpu.VMEM((TILE, BLOCK), jnp.float32),
            pltpu.VMEM((TILE, HALF), jnp.bfloat16),
            pltpu.VMEM((TILE, HALF), jnp.bfloat16),
            pltpu.VMEM((TILE, HALF), jnp.bfloat16),
            pltpu.VMEM((SIDE, SHARD, HALF), jnp.bfloat16),
            pltpu.VMEM((8, 8, TILE), jnp.float32),
            pltpu.VMEM((2, 8, TILE), jnp.float32),
            pltpu.VMEM((TILE, BLOCK), jnp.float32),
            dma((5,)), dma((16,)), dma((16,)), dma((16,)), dma((16,)), dma((16,)), dma((16,)), dma((16,)), dma((16,)),
            dma((3,)), dma((3,)), dma((3,)), dma((3,)), dma((8,)), dma((8,)), dma((4,)), dma((4,)), dma((4,)), dma((4,)),
            dma((4,)), dma((1,)),
        ],
        compiler_params=pltpu.CompilerParams(
            collective_id=0, has_side_effects=True, vmem_limit_bytes=60 * 2**20
        ),
    )(attn_out, out_grad, weight, signs)
    return pl.pallas_call(
        copy_kernel,
        out_shape=tuple(jax.ShapeDtypeStruct(part.shape, part.dtype) for part in made),
        in_specs=[hbm, hbm],
        out_specs=(hbm, hbm),
        scratch_shapes=[
            pltpu.VMEM((TOK, FEATURES), jnp.bfloat16), pltpu.VMEM((SHARD, HALF), jnp.float32), dma((16,))
        ],
    )(*made)


def solution(mesh):
    in_specs = (P(("dp", "fsdp"), None), P(("dp", "fsdp"), None), P("fsdp", None), P())
    out_specs = (P(("dp", "fsdp"), None), P("fsdp", "dp"))
    return jax.shard_map(body, mesh=mesh, in_specs=in_specs, out_specs=out_specs, check_vma=False)
```
